768 devices in a mesh: dp: 12 (over z), cls: 64 (over y, x, core).
Axes of the slice: x: 4, y: 8, z: 12, core: 2. Of those that a mesh axis runs over, the one named last changes fastest.
Arguments:
- features: bfloat16 [3072, 256], P('dp'), may hold values from -1 to 1
- prototypes: bfloat16 [196608, 256], P('cls'), may hold values from -0.101 to 0.101
- prior_counts: int32 [196608], P('cls'), may hold values from 1 to 4096, as said below
- cotangent: bfloat16 [3072, 196608], P('dp', 'cls'), may hold values from -6 to 6
Outputs:
- feature_grad: float32 [3072, 256], P('dp')
- prototype_grad: float32 [196608, 256], P(('cls', 'dp'))
The draws below stay inside these ranges and needn't reach their ends.
Inputs may be any that keep to these rules, and one draw needn't show every extreme that they name: `prior_counts`: counts of the labeled pool for each class, some class holding exactly the maximum.
All inputs are finite; a program needn't handle non-finite values.
Results may differ from the reference program's by a relative error of at most 0.0022.
Values may be sent and summed in bfloat16 or wider, within the bound.
No kernel may reach another device: no remote copies, remote signals or barrier semaphores. Data moves between devices by JAX's collectives and lax.ppermute only.
A program may use at most 32 MiB of HBM per device.

```python
import jax
import jax.numpy as jnp
from jax import lax

D = 256
ROWS = 256
KDEV = 3072
ITERS = 3
N = 3072
K = 196608


def draw_prior_counts(key, part):
    first, second, third = jax.random.split(key, 3)
    level = jax.random.randint(first, (K,), 0, 13)
    picked = jax.random.randint(second, (), 0, K)
    level = jnp.where(jnp.arange(K) == picked, 12, level)
    lowest = jnp.power(2, level).astype(jnp.int32)
    value = jax.random.randint(third, (K,), lowest, 2 * lowest)
    return jnp.minimum(value, 4096).astype(jnp.int32)


def shared_pattern(key):
    pattern_key = jax.random.fold_in(key, 7301)
    signs = jax.random.randint(pattern_key, (D,), 0, 2)
    return (2 * signs - 1).astype(jnp.float32)


def block_levels(key, count):
    first = jax.random.fold_in(key, 0)
    return jax.random.uniform(first, (count,), jnp.float32, -1.0, 1.0)


def unit_noise(key, shape):
    return jax.random.uniform(key, shape, jnp.float32, -1.0, 1.0)


def draw_features(key, part):
    pattern = shared_pattern(key)
    own_key = jax.random.fold_in(key, 1103)
    first, second = jax.random.split(own_key)
    levels = jnp.repeat(block_levels(first, N // ROWS), ROWS)
    noise = unit_noise(second, (N, D))
    values = 0.6 * noise + 0.4 * levels[:, None] * pattern[None, :]
    return values.astype(jnp.bfloat16)


def draw_prototypes(key, part):
    pattern = shared_pattern(key)
    own_key = jax.random.fold_in(key, 2207)
    first, second = jax.random.split(own_key)
    levels = jnp.repeat(block_levels(first, K // KDEV), KDEV)
    noise = unit_noise(second, (K, D))
    values = 0.084 * noise + 0.016 * levels[:, None] * pattern[None, :]
    return values.astype(jnp.bfloat16)


def draw_cotangent(key, part):
    own_key = jax.random.fold_in(key, 3301)
    first, second = jax.random.split(own_key)
    table = jax.random.normal(first, (N // ROWS, K // KDEV), jnp.float32)
    noise = 0.8 * jax.random.normal(second, (N, K), jnp.float32)
    spread = jnp.repeat(jnp.repeat(table, ROWS, axis=0), KDEV, axis=1)
    values = jnp.clip(noise + spread, -6.0, 6.0)
    return values.astype(jnp.bfloat16)


def setup_inputs(seed: int = 0) -> dict:
    keys = jax.random.split(jax.random.key(seed), 5)
    features = draw_features(jax.random.fold_in(keys[4], 71), 0)
    prototypes = draw_prototypes(jax.random.fold_in(keys[4], 71), 0)
    prior_counts = draw_prior_counts(jax.random.fold_in(keys[4], 71), 0)
    cotangent = draw_cotangent(jax.random.fold_in(keys[4], 71), 0)
    return {"features": features, "prototypes": prototypes, "prior_counts": prior_counts, "cotangent": cotangent}


sharpness = 4.0
relax_power = 0.7


def matvec(kernel, vector):
    return jnp.dot(kernel, vector, precision=lax.Precision.HIGHEST)


def vecmat(vector, kernel):
    return jnp.dot(vector, kernel, precision=lax.Precision.HIGHEST)


def reference(features, prototypes, prior_counts, cotangent):
    logits = jnp.einsum("nd,kd->nk", features, prototypes, preferred_element_type=jnp.float32)
    kernel = jnp.exp(sharpness * logits)
    rows_all = kernel.shape[0]
    protos_all = kernel.shape[1]
    total = jnp.sum(prior_counts.astype(jnp.float32))
    target = rows_all * prior_counts.astype(jnp.float32) / total
    vectors_v = [jnp.ones((protos_all,), jnp.float32)]
    vectors_u = []
    sums_x = []
    sums_y = []
    for step in range(ITERS):
        x_now = matvec(kernel, vectors_v[-1])
        u_now = 1.0 / x_now
        y_now = vecmat(u_now, kernel)
        v_now = (target / y_now) ** relax_power
        sums_x.append(x_now)
        sums_y.append(y_now)
        vectors_u.append(u_now)
        vectors_v.append(v_now)
    weighted = protos_all * cotangent.astype(jnp.float32) * kernel
    u_last = vectors_u[-1]
    v_last = vectors_v[-1]
    du_last = matvec(weighted, v_last)
    d_v = vecmat(u_last, weighted)
    dkernel = protos_all * cotangent.astype(jnp.float32) * u_last[:, None] * v_last[None, :]
    for step in range(ITERS - 1, -1, -1):
        d_y = -relax_power * d_v * vectors_v[step + 1] / sums_y[step]
        d_u = matvec(kernel, d_y)
        if step == ITERS - 1:
            d_u = du_last + d_u
        d_x = -d_u * vectors_u[step] / sums_x[step]
        if step > 0:
            d_v = vecmat(d_x, kernel)
        dkernel = dkernel + vectors_u[step][:, None] * d_y[None, :] + d_x[:, None] * vectors_v[step][None, :]
    dlogits = (sharpness * kernel * dkernel).astype(jnp.bfloat16)
    feature_grad = jnp.dot(dlogits, prototypes, preferred_element_type=jnp.float32)
    prototype_grad = jnp.einsum("nk,nd->kd", dlogits, features, preferred_element_type=jnp.float32)
    return feature_grad, prototype_grad
```

```python
import jax
import jax.numpy as jnp
from jax import lax
from jax.sharding import PartitionSpec as P

ITERS = 3


sharpness = 4.0
relax_power = 0.7


def matvec(kernel, vector):
    return jnp.dot(kernel, vector, precision=lax.Precision.HIGHEST)


def vecmat(vector, kernel):
    return jnp.dot(vector, kernel, precision=lax.Precision.HIGHEST)


def exchange_total(partial, axis):
    size = lax.axis_size(axis)
    copies = jnp.broadcast_to(partial[None], (size,) + partial.shape)
    return jnp.sum(lax.all_to_all(copies, axis, 0, 0), axis=0)


def row_total(partial_rows):
    return exchange_total(partial_rows, "cls")


def column_total(partial_columns):
    return exchange_total(partial_columns, "dp")


def per_device(features, prototypes, prior_counts, cotangent):
    rows, width = features.shape
    columns = prototypes.shape[0]
    samples = lax.axis_size("dp")
    classes = lax.axis_size("cls")
    own = columns // samples
    features_all = lax.all_gather(features, "dp", axis=0, tiled=True)
    cotangent_columns = lax.all_to_all(cotangent, "dp", 1, 0, tiled=True)
    logits = jnp.einsum("nd,kd->nk", features, prototypes, preferred_element_type=jnp.float32)
    kernel = jnp.exp(sharpness * logits)
    rows_all = rows * samples
    protos_all = columns * classes
    counts = prior_counts.astype(jnp.float32)
    vectors_v = [jnp.ones((columns,), jnp.float32)]
    vectors_u = []
    sums_x = []
    sums_y = []
    total = jnp.sum(counts)
    for step in range(ITERS):
        partial = matvec(kernel, vectors_v[-1])
        if step == 0:
            partial = jnp.concatenate([partial, jnp.full((128,), total)])
        x_now = row_total(partial)
        if step == 0:
            target = rows_all * counts / x_now[rows]
            x_now = x_now[:rows]
        u_now = 1.0 / x_now
        if step < ITERS - 1:
            y_now = column_total(vecmat(u_now, kernel))
        else:
            scaled_grad = protos_all * cotangent.astype(jnp.float32)
            weighted = scaled_grad * kernel
            both = column_total(jnp.stack([vecmat(u_now, kernel), vecmat(u_now, weighted)]))
            y_now, d_v = both[0], both[1]
        v_now = (target / y_now) ** relax_power
        sums_x.append(x_now)
        sums_y.append(y_now)
        vectors_u.append(u_now)
        vectors_v.append(v_now)
    du_local = matvec(weighted, vectors_v[-1])
    dys = [None] * ITERS
    dxs = [None] * ITERS
    for step in range(ITERS - 1, -1, -1):
        d_y = -relax_power * d_v * vectors_v[step + 1] / sums_y[step]
        partial_u = matvec(kernel, d_y)
        if step == ITERS - 1:
            partial_u = du_local + partial_u
        d_u = row_total(partial_u)
        d_x = -d_u * vectors_u[step] / sums_x[step]
        if step > 0:
            d_v = column_total(vecmat(d_x, kernel))
        dys[step] = d_y
        dxs[step] = d_x
    dkernel = scaled_grad * vectors_u[-1][:, None] * vectors_v[-1][None, :]
    for step in range(ITERS - 1, -1, -1):
        dkernel = dkernel + vectors_u[step][:, None] * dys[step][None, :] + dxs[step][:, None] * vectors_v[step][None, :]
    dlogits = (sharpness * kernel * dkernel).astype(jnp.bfloat16)
    partial = jnp.dot(dlogits, prototypes, preferred_element_type=jnp.float32)
    slices = lax.all_to_all(partial.reshape(classes, rows // classes * width), "cls", 0, 0)
    mine = jnp.sum(slices, axis=0)
    feature_grad = lax.all_to_all(jnp.broadcast_to(mine[None], slices.shape), "cls", 0, 0).reshape(rows, width)

    left = lax.dynamic_slice_in_dim
    start = lax.axis_index("dp") * own
    rows_u = jnp.stack(vectors_u + dxs)
    rows_u = lax.all_gather(rows_u, "dp", axis=1, tiled=True)
    own_protos = left(prototypes, start, own, 0)
    vs = [left(v, start, own, 0) for v in vectors_v]
    dy = [left(v, start, own, 0) for v in dys]
    logits_c = jnp.einsum("nd,kd->nk", features_all, own_protos, preferred_element_type=jnp.float32)
    kernel_c = jnp.exp(sharpness * logits_c)
    dkernel_c = protos_all * cotangent_columns.astype(jnp.float32) * rows_u[ITERS - 1][:, None] * vs[-1][None, :]
    for step in range(ITERS - 1, -1, -1):
        dkernel_c = dkernel_c + rows_u[step][:, None] * dy[step][None, :] + rows_u[ITERS + step][:, None] * vs[step][None, :]
    dlogits_c = (sharpness * kernel_c * dkernel_c).astype(jnp.bfloat16)
    prototype_grad = lax.dot_general(
        dlogits_c, features_all, (((0,), (0,)), ((), ())), preferred_element_type=jnp.float32
    )
    return (feature_grad, prototype_grad)


def solution(mesh):
    return jax.shard_map(
        per_device,
        mesh=mesh,
        in_specs=(P("dp", None), P("cls", None), P("cls"), P("dp", "cls")),
        out_specs=(P("dp", None), P(("cls", "dp"), None)),
        check_vma=False,
    )
```

```python
import functools

import jax
import jax.numpy as jnp
from jax import lax
from jax.experimental import pallas as pl
from jax.experimental.pallas import tpu as pltpu
from jax.sharding import PartitionSpec as P

sharpness = 4.0
relax_power = 0.7

LANES = 128
F32 = jnp.float32
BF16 = jnp.bfloat16


def call(body, outs, args, name, smem=0, flops=0):
    specs = [pl.BlockSpec(memory_space=pltpu.SMEM)] * smem
    specs += [pl.BlockSpec(memory_space=pltpu.VMEM)] * (len(args) - smem)
    moved = sum(a.size * a.dtype.itemsize for a in (*args, *outs))
    return pl.pallas_call(
        body,
        out_shape=outs,
        in_specs=specs,
        out_specs=[pl.BlockSpec(memory_space=pltpu.VMEM)] * len(outs),
        compiler_params=pltpu.CompilerParams(vmem_limit_bytes=16 * 2**20),
        cost_estimate=pl.CostEstimate(flops=flops, bytes_accessed=moved, transcendentals=0),
        name=name,
    )(*args)


def f32(*shape):
    return jax.ShapeDtypeStruct(shape, F32)


def tiles(size, width):
    return [slice(start, start + width) for start in range(0, size, width)]


def down(row, width=LANES):
    return jnp.transpose(jnp.broadcast_to(row, (width, row.shape[1])))


def flat(sums):
    return jnp.sum(jnp.transpose(sums), axis=0, keepdims=True)


def copies(row, count):
    return jnp.broadcast_to(row[None], (count,) + row.shape)


def parts(value):
    high = value.astype(BF16)
    return high, (value - high.astype(F32)).astype(BF16)


def rows_of(kernel_ref, weight):
    sums = 0.0
    for at in tiles(kernel_ref.shape[1], LANES):
        sums = sums + kernel_ref[:, at] * weight(at)
    return flat(sums)


def received(ref, start, stop):
    return jnp.sum(ref[:, :, start:stop], axis=0)


def expo_body(left_ref, right_ref, kernel_ref):
    left = left_ref[...]
    for at in tiles(right_ref.shape[0], 512):
        logits = lax.dot_general(left, right_ref[at, :], (((1,), (1,)), ((), ())), preferred_element_type=F32)
        kernel_ref[:, at] = jnp.exp(sharpness * logits)


def start_body(features_ref, prototypes_ref, counts_ref, kernel_ref, out_ref):
    rows = features_ref.shape[0]
    left = features_ref[...]
    sums = 0.0
    for at in tiles(prototypes_ref.shape[0], 512):
        logits = lax.dot_general(left, prototypes_ref[at, :], (((1,), (1,)), ((), ())), preferred_element_type=F32)
        block = jnp.exp(sharpness * logits)
        kernel_ref[:, at] = block
        for inner in tiles(512, LANES):
            sums = sums + block[:, inner]
    out_ref[:, :, :rows] = copies(flat(sums), out_ref.shape[0])
    total = jnp.sum(counts_ref[...].astype(F32), axis=1, keepdims=True)
    out_ref[:, :, rows:] = jnp.broadcast_to(total[None], (out_ref.shape[0], 1, LANES))


def columns_body(first, x_ref, kernel_ref, *rest):
    if first:
        total_ref, u_ref, out_ref = rest
    else:
        u_ref, out_ref = rest
    rows, columns = kernel_ref.shape
    count = out_ref.shape[0]
    u = 1.0 / received(x_ref, 0, rows)
    u_ref[...] = u
    if first:
        total_ref[...] = received(x_ref, rows, rows + LANES)
    wide = down(u)
    for at in tiles(columns, LANES):
        out_ref[:, :, at] = copies(jnp.sum(kernel_ref[:, at] * wide, axis=0, keepdims=True), count)
    out_ref[:, :, columns:] = copies(u, count)


def columns_last_body(protos_all, x_ref, kernel_ref, cotangent_ref, u_ref, out_ref):
    rows, columns = kernel_ref.shape
    count = out_ref.shape[0]
    u = 1.0 / received(x_ref, 0, rows)
    u_ref[...] = u
    wide = down(u)
    for at in tiles(columns, LANES):
        weighted = kernel_ref[:, at] * wide
        out_ref[:, :, at] = copies(jnp.sum(weighted, axis=0, keepdims=True), count)
        weighted = weighted * cotangent_ref[:, at].astype(F32)
        later = slice(columns + at.start, columns + at.stop)
        out_ref[:, :, later] = copies(protos_all * jnp.sum(weighted, axis=0, keepdims=True), count)
    out_ref[:, :, 2 * columns :] = copies(u, count)


def spread(ref, all_ref, start):
    rows = all_ref.shape[1] // ref.shape[0]
    for i in range(ref.shape[0]):
        all_ref[:, i * rows : (i + 1) * rows] = ref[i, :, start : start + rows]


def relaxed(y, counts_ref, total_ref, samples_all):
    target = samples_all * counts_ref[...].astype(F32) / total_ref[:, :1]
    return jnp.exp(relax_power * jnp.log(target / y))


def rows_body(samples_all, y_ref, counts_ref, total_ref, kernel_ref, y_out_ref, v_ref, all_ref, out_ref):
    columns = kernel_ref.shape[1]
    y = received(y_ref, 0, columns)
    y_out_ref[...] = y
    v_ref[...] = relaxed(y, counts_ref, total_ref, samples_all)
    spread(y_ref, all_ref, columns)
    out_ref[...] = copies(rows_of(kernel_ref, lambda at: v_ref[:, at]), out_ref.shape[0])


def rows_last_body(
    samples_all, protos_all, y_ref, counts_ref, total_ref, kernel_ref, cotangent_ref, v_ref, dy_ref, all_ref, out_ref
):
    columns = kernel_ref.shape[1]
    y = received(y_ref, 0, columns)
    v = relaxed(y, counts_ref, total_ref, samples_all)
    v_ref[...] = v
    dy_ref[...] = -relax_power * received(y_ref, columns, 2 * columns) * v / y
    spread(y_ref, all_ref, 2 * columns)
    weight = lambda at: protos_all * cotangent_ref[:, at].astype(F32) * v_ref[:, at] + dy_ref[:, at]
    out_ref[...] = copies(rows_of(kernel_ref, weight), out_ref.shape[0])


def back_columns_body(has_slice, du_ref, u_ref, kernel_ref, *rest):
    if has_slice:
        dx_ref, slice_ref, out_ref = rest
    else:
        dx_ref, out_ref = rest
    rows, columns = kernel_ref.shape
    count = out_ref.shape[0]
    u = u_ref[...]
    dx = -received(du_ref, 0, rows) * u * u
    dx_ref[...] = dx
    if has_slice:
        slice_ref[...] = received(du_ref, rows, du_ref.shape[2])
    wide = down(dx)
    for at in tiles(columns, LANES):
        out_ref[:, :, at] = copies(jnp.sum(kernel_ref[:, at] * wide, axis=0, keepdims=True), count)
    out_ref[:, :, columns:] = copies(dx, count)


def back_rows_body(dv_ref, v_ref, y_ref, kernel_ref, extra_ref, dy_ref, all_ref, out_ref):
    rows, columns = kernel_ref.shape
    dy_ref[...] = -relax_power * received(dv_ref, 0, columns) * v_ref[...] / y_ref[...]
    spread(dv_ref, all_ref, columns)
    row = rows_of(kernel_ref, lambda at: dy_ref[:, at])
    out_ref[:, :, :rows] = copies(row, out_ref.shape[0])
    out_ref[:, :, rows:] = extra_ref[...]


def scatter_rows(value, out_ref, start):
    count = out_ref.shape[0]
    width = value.shape[1]
    for r in range(value.shape[0] // count):
        block = value[r * count : (r + 1) * count, :]
        out_ref[:, :, start + r * width : start + (r + 1) * width] = block[:, None, :]


def product(value, right):
    high, low = parts(value)
    return jnp.dot(high, right, preferred_element_type=F32) + jnp.dot(low, right, preferred_element_type=F32)


def plain_product_body(kernel_ref, prototypes_ref, out_ref):
    total = 0.0
    for at in tiles(kernel_ref.shape[1], 512):
        total = total + product(kernel_ref[:, at], prototypes_ref[at, :])
    scatter_rows(sharpness * total, out_ref, 0)


def known_product_body(
    protos_all, kernel_ref, cotangent_ref, prototypes_ref, u2_ref, u3_ref, dx2_ref, dx3_ref,
    v1_ref, v2_ref, v3_ref, dy2_ref, dy3_ref, out_ref,
):
    width = 256
    u2, u3, dx2, dx3 = (down(ref[...], width) for ref in (u2_ref, u3_ref, dx2_ref, dx3_ref))
    total = 0.0
    for at in tiles(kernel_ref.shape[1], width):
        grad = protos_all * cotangent_ref[:, at].astype(F32)
        inner = u3 * (grad * v3_ref[:, at] + dy3_ref[:, at])
        inner = inner + dx3 * v2_ref[:, at] + u2 * dy2_ref[:, at] + dx2 * v1_ref[:, at]
        total = total + product(kernel_ref[:, at] * inner, prototypes_ref[at, :])
    out_ref[...] = sharpness * total


def last_rows_body(dv_ref, v_ref, y_ref, kernel_ref, prototypes_ref, known_ref, u_ref, dy_ref, all_ref, out_ref):
    rows, columns = kernel_ref.shape
    dy_ref[...] = -relax_power * received(dv_ref, 0, columns) * v_ref[...] / y_ref[...]
    spread(dv_ref, all_ref, columns)
    width = 256
    sums, total = 0.0, 0.0
    for at in tiles(columns, width):
        weighted = kernel_ref[:, at] * dy_ref[:, at]
        for inner in tiles(width, LANES):
            sums = sums + weighted[:, inner]
        total = total + product(weighted, prototypes_ref[at, :])
    out_ref[:, :, :rows] = copies(flat(sums), out_ref.shape[0])
    total = known_ref[...] + sharpness * down(u_ref[...], total.shape[1]) * total
    scatter_rows(total, out_ref, rows)


def finish_rows_body(place_ref, du_ref, u_ref, slice_ref, dx_out_ref, out_ref):
    rows = u_ref.shape[1]
    u = u_ref[...]
    dx = -received(du_ref, 0, rows) * u * u
    dx_out_ref[...] = copies(dx, dx_out_ref.shape[0])
    count = out_ref.shape[0]
    mine = received(du_ref, rows, du_ref.shape[2])
    width = mine.shape[1] * count // rows
    lane = lax.broadcasted_iota(jnp.int32, dx.shape, 1)
    for r in range(rows // count):
        at = slice(r * width, (r + 1) * width)
        value = jnp.sum(jnp.where(lane == r * count + place_ref[0], dx, 0.0), axis=1, keepdims=True)
        out_ref[:, :, at] = copies(mine[:, at] + value * slice_ref[:, at], count)


def weighted_product_body(protos_all, kernel_ref, cotangent_ref, u_ref, features_ref, out_ref):
    width = 256
    wide = protos_all * down(u_ref[...], width)
    features = features_ref[...]
    rows = (((0,), (0,)), ((), ()))
    for at in tiles(kernel_ref.shape[1], width):
        high, low = parts(kernel_ref[:, at] * cotangent_ref[:, at].astype(F32) * wide)
        out_ref[at, :] = lax.dot_general(high, features, rows, preferred_element_type=F32) + lax.dot_general(
            low, features, rows, preferred_element_type=F32
        )


def own_columns(place_ref, ref, own, width=LANES):
    start = pl.multiple_of(place_ref[0] * own, own)
    return down(ref[:, pl.ds(start, own)], width)


def known_columns_body(
    place_ref, kernel_ref, u1_ref, u2_ref, u3_ref, dx2_ref, dx3_ref, v1_ref, v2_ref, dy1_ref, dy2_ref, dy3_ref, out_ref
):
    own, samples = kernel_ref.shape
    v1, v2, dy1, dy2, dy3 = (own_columns(place_ref, ref, own) for ref in (v1_ref, v2_ref, dy1_ref, dy2_ref, dy3_ref))
    for at in tiles(samples, LANES):
        inner = u3_ref[:, at] * dy3 + dx3_ref[:, at] * v2
        inner = inner + u2_ref[:, at] * dy2 + dx2_ref[:, at] * v1 + u1_ref[:, at] * dy1
        out_ref[:, at] = sharpness * kernel_ref[:, at] * inner


def finish_columns_body(place_ref, dx_ref, kernel_ref, known_ref, features_ref, v_ref, weighted_ref, out_ref):
    own = kernel_ref.shape[0]
    rows = dx_ref.shape[2]
    total = sharpness * own_columns(place_ref, v_ref, own, out_ref.shape[1]) * weighted_ref[...]
    for i in range(dx_ref.shape[0]):
        at = slice(i * rows, (i + 1) * rows)
        dlogits = known_ref[:, at] + sharpness * kernel_ref[:, at] * dx_ref[i]
        total = total + product(dlogits, features_ref[at, :])
    out_ref[...] = total


def gather_rows_body(ref, out_ref):
    count = ref.shape[0]
    width = out_ref.shape[1]
    for r in range(out_ref.shape[0] // count):
        out_ref[r * count : (r + 1) * count, :] = ref[:, 0, r * width : (r + 1) * width]


def exchange(messages, axis):
    return lax.all_to_all(messages, axis, 0, 0, tiled=True)


def together(*arrays):
    return lax.optimization_barrier(arrays)


def per_device(features, prototypes, prior_counts, cotangent):
    rows, width = features.shape
    columns = prototypes.shape[0]
    samples = lax.axis_size("dp")
    classes = lax.axis_size("cls")
    own = columns // samples
    rows_all = rows * samples
    protos_all = float(columns * classes)
    sliced = rows * width // classes
    counts = prior_counts.reshape(1, columns)
    dp_place = lax.axis_index("dp").astype(jnp.int32).reshape(1)
    cls_place = lax.axis_index("cls").astype(jnp.int32).reshape(1)
    block_flops = 2 * rows * columns

    features_all = lax.all_gather(features, "dp", axis=0, tiled=True)

    row, column = f32(1, rows), f32(1, columns)
    everyone = f32(1, rows_all)
    kernel, message = call(
        start_body, [f32(rows, columns), f32(classes, 1, rows + LANES)], [features, prototypes, counts], "start",
        flops=block_flops * width,
    )
    u, v, y, u_all = [], [], [], []
    for step in range(2):
        x_message = exchange(message, "cls")
        outs = [row, f32(samples, 1, columns + rows)]
        if step == 0:
            total, u_now, message = call(
                functools.partial(columns_body, True), [f32(1, LANES)] + outs, [x_message, kernel], "columns_first", flops=block_flops
            )
        else:
            u_now, message = call(functools.partial(columns_body, False), outs, [x_message, kernel], "columns", flops=block_flops)
        y_message = exchange(message, "dp")
        y_now, v_now, all_now, message = call(
            functools.partial(rows_body, float(rows_all)), [column, column, everyone, f32(classes, 1, rows)],
            [y_message, counts, total, kernel], "rows", flops=block_flops,
        )
        u.append(u_now)
        v.append(v_now)
        y.append(y_now)
        u_all.append(all_now)
    x_message = exchange(message, "cls")
    x_message, features_all = together(x_message, features_all)
    u_now, message = call(
        functools.partial(columns_last_body, protos_all), [row, f32(samples, 1, 2 * columns + rows)],
        [x_message, kernel, cotangent], "columns_last", flops=2 * block_flops,
    )
    u.append(u_now)
    message, u_late = together(message, u_now)
    (weighted,) = call(
        functools.partial(weighted_product_body, protos_all), [f32(columns, width)], [kernel, cotangent, u_late, features],
        "weighted_product", flops=2 * block_flops * width,
    )
    y_message, weighted = together(exchange(message, "dp"), weighted)
    weighted = lax.psum_scatter(weighted, "dp", scatter_dimension=0, tiled=True)
    v_now, dy3, all_now, message = call(
        functools.partial(rows_last_body, float(rows_all), protos_all),
        [column, column, everyone, f32(classes, 1, rows)],
        [y_message, counts, total, kernel, cotangent], "rows_last", flops=2 * block_flops,
    )
    v.append(v_now)
    u_all.append(all_now)

    message, right = together(message, prototypes)
    (plain,) = call(plain_product_body, [f32(classes, 1, sliced)], [kernel, right], "plain_product", flops=2 * block_flops * width)
    du_message, plain = together(exchange(message, "cls"), plain)
    dx3, message = call(
        functools.partial(back_columns_body, False), [row, f32(samples, 1, columns + rows)], [du_message, u[2], kernel],
        "back_columns", flops=block_flops,
    )
    message, right = together(message, features_all)
    own_prototypes = lax.dynamic_slice_in_dim(prototypes, dp_place[0] * own, own, 0)
    (kernel_columns,) = call(expo_body, [f32(own, rows_all)], [own_prototypes, right], "expo", flops=block_flops * width)
    dv_message, kernel_columns = together(exchange(message, "dp"), kernel_columns)
    dy2, dx3_all, message = call(
        back_rows_body, [column, everyone, f32(classes, 1, rows + sliced)], [dv_message, v[1], y[1], kernel, plain],
        "back_rows", flops=block_flops,
    )
    du_message = exchange(message, "cls")
    dx2, plain_slice, message = call(
        functools.partial(back_columns_body, True), [row, f32(1, sliced), f32(samples, 1, columns + rows)],
        [du_message, u[1], kernel], "back_columns_slice", flops=block_flops,
    )
    message, dx2_late = together(message, dx2)
    (known,) = call(
        functools.partial(known_product_body, protos_all), [f32(rows, width)],
        [kernel, cotangent, prototypes, u[1], u[2], dx2_late, dx3, v[0], v[1], v[2], dy2, dy3], "known_product",
        flops=2 * block_flops * width,
    )
    dv_message, known = together(exchange(message, "dp"), known)
    dy1, dx2_all, message = call(
        last_rows_body, [column, everyone, f32(classes, 1, rows + sliced)],
        [dv_message, v[0], y[0], kernel, prototypes, known, u[0]], "last_rows", flops=2 * block_flops * width,
    )
    message, dy1 = together(message, dy1)
    (known_columns,) = call(
        known_columns_body, [f32(own, rows_all)],
        [dp_place, kernel_columns, *u_all, dx2_all, dx3_all, v[0], v[1], dy1, dy2, dy3], "known_columns",
        smem=1, flops=20 * own * rows_all,
    )
    du_message, known_columns = together(exchange(message, "cls"), known_columns)
    dx_message, message = call(
        finish_rows_body, [f32(samples, 1, rows), f32(classes, 1, sliced)], [cls_place, du_message, u[0], plain_slice],
        "finish_rows", smem=1,
    )
    dx1 = exchange(dx_message, "dp")
    gathered = exchange(message, "cls")
    (prototype_grad,) = call(
        finish_columns_body, [f32(own, width)],
        [dp_place, dx1, kernel_columns, known_columns, features_all, v[2], weighted], "finish_columns", smem=1,
        flops=2 * block_flops * width,
    )
    (feature_grad,) = call(gather_rows_body, [f32(rows, width)], [gathered], "gather_rows")
    return (feature_grad, prototype_grad)


def solution(mesh):
    return jax.shard_map(
        per_device,
        mesh=mesh,
        in_specs=(P("dp", None), P("cls", None), P("cls"), P("dp", "cls")),
        out_specs=(P("dp", None), P(("cls", "dp"), None)),
        check_vma=False,
    )
```

```python
import functools

import jax
import jax.numpy as jnp
from jax import lax
from jax.experimental import pallas as pl
from jax.experimental.pallas import tpu as pltpu
from jax.sharding import PartitionSpec as P

sharpness = 4.0
relax_power = 0.7

LANES = 128
F32 = jnp.float32
BF16 = jnp.bfloat16


def call(body, outs, args, name, smem=0, flops=0):
    specs = [pl.BlockSpec(memory_space=pltpu.SMEM)] * smem
    specs += [pl.BlockSpec(memory_space=pltpu.VMEM)] * (len(args) - smem)
    moved = sum(a.size * a.dtype.itemsize for a in (*args, *outs))
    return pl.pallas_call(
        body,
        out_shape=outs,
        in_specs=specs,
        out_specs=[pl.BlockSpec(memory_space=pltpu.VMEM)] * len(outs),
        compiler_params=pltpu.CompilerParams(vmem_limit_bytes=24 * 2**20),
        cost_estimate=pl.CostEstimate(flops=flops, bytes_accessed=moved, transcendentals=0),
        name=name,
    )(*args)


def f32(*shape):
    return jax.ShapeDtypeStruct(shape, F32)


def tiles(size, width):
    return [slice(start, start + width) for start in range(0, size, width)]


def down(row, width=LANES):
    return jnp.transpose(jnp.broadcast_to(row, (width, row.shape[1])))


def flat(sums):
    return jnp.sum(jnp.transpose(sums), axis=0, keepdims=True)


def copies(row, count):
    return jnp.broadcast_to(row[None], (count,) + row.shape)


def parts(value):
    high = value.astype(BF16)
    return high, (value - high.astype(F32)).astype(BF16)


def rows_of(kernel_ref, weight):
    sums = 0.0
    for at in tiles(kernel_ref.shape[1], LANES):
        sums = sums + kernel_ref[:, at] * weight(at)
    return flat(sums)


def received(ref, start, stop):
    return jnp.sum(ref[:, :, start:stop], axis=0)


V, Y, TARGET, DY = (0, 1, 2), (3, 4), 5, (3, 4, 5)
U, DX, PLAIN = (0, 1, 2), (None, 4, 3), 8


def carry(old_ref, new_ref):
    new_ref[...] = old_ref[...]


def put(ref, row, value):
    ref[row : row + 1, :] = value


def get(ref, row, at=slice(None)):
    return ref[row : row + 1, at]


def exponential(left, right):
    logits = lax.dot_general(left, right, (((1,), (1,)), ((), ())), preferred_element_type=F32)
    return jnp.exp(sharpness * logits)


def start_body(features_ref, prototypes_ref, counts_ref, kernel_ref, cols_ref, out_ref):
    rows = features_ref.shape[0]
    width = 512
    left = features_ref[...]
    sums, plain = 0.0, 0.0
    for at in tiles(prototypes_ref.shape[0], width):
        right = prototypes_ref[at, :]
        block = exponential(left, right)
        kernel_ref[:, at] = block
        for inner in tiles(width, LANES):
            sums = sums + block[:, inner]
        plain = plain + product(block, right)
    out_ref[:, :, :rows] = copies(flat(sums), out_ref.shape[0])
    scatter_rows(sharpness * plain, out_ref, rows + LANES)
    counts = counts_ref[...].astype(F32)
    cols_ref[...] = jnp.zeros_like(cols_ref)
    put(cols_ref, TARGET, counts)
    total = jnp.sum(counts, axis=1, keepdims=True)
    out_ref[:, :, rows : rows + LANES] = jnp.broadcast_to(total[None], (out_ref.shape[0], 1, LANES))


def column_sums(kernel_ref, row, out_ref):
    columns = kernel_ref.shape[1]
    count = out_ref.shape[0]
    wide = down(row)
    for at in tiles(columns, LANES):
        out_ref[:, :, at] = copies(jnp.sum(kernel_ref[:, at] * wide, axis=0, keepdims=True), count)
    out_ref[:, :, columns:] = copies(row, count)


def columns_first_body(samples_all, x_ref, kernel_ref, cols_ref, cols_out, rws_out, every_out, out_ref):
    rows = kernel_ref.shape[0]
    u = 1.0 / received(x_ref, 0, rows)
    column_sums(kernel_ref, u, out_ref)
    total = received(x_ref, rows, rows + LANES)[:, :1]
    carry(cols_ref, cols_out)
    put(cols_out, TARGET, samples_all * get(cols_ref, TARGET) / total)
    rws_out[...] = jnp.zeros_like(rws_out)
    put(rws_out, U[0], u)
    for i, at in enumerate(tiles(x_ref.shape[2] - rows - LANES, rows)):
        put(rws_out, PLAIN + i, received(x_ref, rows + LANES + at.start, rows + LANES + at.stop))
    every_out[...] = jnp.zeros_like(every_out)


def columns_body(step, x_ref, kernel_ref, rws_ref, rws_out, out_ref):
    u = 1.0 / received(x_ref, 0, kernel_ref.shape[0])
    carry(rws_ref, rws_out)
    put(rws_out, U[step], u)
    column_sums(kernel_ref, u, out_ref)


def columns_last_body(step, protos_all, x_ref, kernel_ref, cotangent_ref, rws_ref, rws_out, out_ref):
    rows, columns = kernel_ref.shape
    count = out_ref.shape[0]
    u = 1.0 / received(x_ref, 0, rows)
    carry(rws_ref, rws_out)
    put(rws_out, U[step], u)
    wide = down(u)
    for at in tiles(columns, LANES):
        weighted = kernel_ref[:, at] * wide
        out_ref[:, :, at] = copies(jnp.sum(weighted, axis=0, keepdims=True), count)
        weighted = weighted * cotangent_ref[:, at].astype(F32)
        later = slice(columns + at.start, columns + at.stop)
        out_ref[:, :, later] = copies(protos_all * jnp.sum(weighted, axis=0, keepdims=True), count)
    out_ref[:, :, 2 * columns :] = copies(u, count)


def spread(ref, every_ref, every_out, row, start):
    carry(every_ref, every_out)
    rows = every_out.shape[1] // ref.shape[0]
    for i in range(ref.shape[0]):
        every_out[row : row + 1, i * rows : (i + 1) * rows] = ref[i, :, start : start + rows]


def relaxed(y, cols_ref):
    return jnp.exp(relax_power * jnp.log(get(cols_ref, TARGET) / y))


def rows_body(step, y_ref, kernel_ref, cols_ref, every_ref, cols_out, every_out, out_ref):
    columns = kernel_ref.shape[1]
    y = received(y_ref, 0, columns)
    carry(cols_ref, cols_out)
    put(cols_out, Y[step], y)
    put(cols_out, V[step], relaxed(y, cols_ref))
    spread(y_ref, every_ref, every_out, U[step], columns)
    out_ref[...] = copies(rows_of(kernel_ref, lambda at: get(cols_out, V[step], at)), out_ref.shape[0])


def rows_last_body(step, protos_all, y_ref, kernel_ref, cotangent_ref, cols_ref, every_ref, cols_out, every_out, out_ref):
    columns = kernel_ref.shape[1]
    y = received(y_ref, 0, columns)
    v = relaxed(y, cols_ref)
    carry(cols_ref, cols_out)
    put(cols_out, V[step], v)
    put(cols_out, DY[step], -relax_power * received(y_ref, columns, 2 * columns) * v / y)
    spread(y_ref, every_ref, every_out, U[step], 2 * columns)

    def weight(at):
        return protos_all * cotangent_ref[:, at].astype(F32) * get(cols_out, V[step], at) + get(cols_out, DY[step], at)

    out_ref[...] = copies(rows_of(kernel_ref, weight), out_ref.shape[0])


def back_columns_body(step, du_ref, kernel_ref, rws_ref, rws_out, out_ref):
    u = get(rws_ref, U[step])
    dx = -received(du_ref, 0, kernel_ref.shape[0]) * u * u
    carry(rws_ref, rws_out)
    put(rws_out, DX[step], dx)
    column_sums(kernel_ref, dx, out_ref)


def column_step(step, dv_ref, cols_ref, every_ref, cols_out, every_out):
    columns = cols_ref.shape[1]
    carry(cols_ref, cols_out)
    dy = -relax_power * received(dv_ref, 0, columns) * get(cols_ref, V[step]) / get(cols_ref, Y[step])
    put(cols_out, DY[step], dy)
    spread(dv_ref, every_ref, every_out, DX[step + 1], columns)


def back_rows_body(step, dv_ref, kernel_ref, cols_ref, every_ref, cols_out, every_out, out_ref):
    column_step(step, dv_ref, cols_ref, every_ref, cols_out, every_out)
    out_ref[...] = copies(rows_of(kernel_ref, lambda at: get(cols_out, DY[step], at)), out_ref.shape[0])


def scatter_rows(value, out_ref, start):
    count = out_ref.shape[0]
    width = value.shape[1]
    for r in range(value.shape[0] // count):
        block = value[r * count : (r + 1) * count, :]
        out_ref[:, :, start + r * width : start + (r + 1) * width] = block[:, None, :]


def product(value, right):
    high, low = parts(value)
    return jnp.dot(high, right, preferred_element_type=F32) + jnp.dot(low, right, preferred_element_type=F32)


def cotangent_products_body(
    protos_all, kernel_ref, cotangent_ref, features_ref, prototypes_ref, cols_ref, rws_ref, weighted_ref, known_ref
):
    width = 256
    u3 = down(get(rws_ref, U[2]), width)
    features = features_ref[...]
    rows = (((0,), (0,)), ((), ()))
    total = 0.0
    for at in tiles(kernel_ref.shape[1], width):
        block = kernel_ref[:, at] * u3
        weighted = protos_all * cotangent_ref[:, at].astype(F32) * block
        high, low = parts(weighted)
        weighted_ref[at, :] = lax.dot_general(high, features, rows, preferred_element_type=F32) + lax.dot_general(
            low, features, rows, preferred_element_type=F32
        )
        known = weighted * get(cols_ref, V[2], at) + block * get(cols_ref, DY[2], at)
        total = total + product(known, prototypes_ref[at, :])
    known_ref[...] = total


def last_rows_body(
    dv_ref, kernel_ref, prototypes_ref, known_ref, cols_ref, rws_ref, every_ref, cols_out, every_out, out_ref
):
    rows, columns = kernel_ref.shape
    column_step(0, dv_ref, cols_ref, every_ref, cols_out, every_out)
    width = 256
    u1, u2, dx2, dx3 = (down(get(rws_ref, row), width) for row in (U[0], U[1], DX[1], DX[2]))
    sums, total = 0.0, known_ref[...]
    for at in tiles(columns, width):
        block = kernel_ref[:, at]
        dy1 = get(cols_out, DY[0], at)
        weighted = block * dy1
        for inner in tiles(width, LANES):
            sums = sums + weighted[:, inner]
        inner = u1 * dy1 + u2 * get(cols_out, DY[1], at) + dx2 * get(cols_out, V[0], at) + dx3 * get(cols_out, V[1], at)
        total = total + product(block * inner, prototypes_ref[at, :])
    out_ref[:, :, :rows] = copies(flat(sums), out_ref.shape[0])
    scatter_rows(sharpness * total, out_ref, rows)


def finish_rows_body(place_ref, du_ref, rws_ref, dx_out_ref, out_ref):
    rows = rws_ref.shape[1]
    u = get(rws_ref, U[0])
    dx = -received(du_ref, 0, rows) * u * u
    dx_out_ref[...] = copies(dx, dx_out_ref.shape[0])
    count = out_ref.shape[0]
    mine = received(du_ref, rows, du_ref.shape[2])
    width = mine.shape[1] * count // rows
    lane = lax.broadcasted_iota(jnp.int32, dx.shape, 1)
    for r in range(rows // count):
        at = slice(r * width, (r + 1) * width)
        value = jnp.sum(jnp.where(lane == r * count + place_ref[0], dx, 0.0), axis=1, keepdims=True)
        out_ref[:, :, at] = copies(mine[:, at] + value * get(rws_ref, PLAIN + r), count)


def own_rows(place_ref, size):
    return pl.ds(pl.multiple_of(place_ref[0] * size, size), size)


def known_columns_body(place_ref, prototypes_ref, features_ref, cols_ref, every_ref, out_ref):
    own, samples = out_ref.shape
    left = prototypes_ref[own_rows(place_ref, own), :]
    mine = cols_ref[:, own_rows(place_ref, own)]
    width = 256
    v1, v2, dy1, dy2, dy3 = (down(mine[row : row + 1, :], width) for row in (V[0], V[1], DY[0], DY[1], DY[2]))
    for at in tiles(samples, width):
        inner = get(every_ref, U[2], at) * dy3 + get(every_ref, DX[2], at) * v2
        inner = inner + get(every_ref, U[1], at) * dy2 + get(every_ref, DX[1], at) * v1 + get(every_ref, U[0], at) * dy1
        out_ref[:, at] = inner * exponential(left, features_ref[at, :])


def finish_columns_body(place_ref, dx_ref, known_ref, prototypes_ref, features_ref, cols_ref, weighted_ref, out_ref):
    own = known_ref.shape[0]
    rows = dx_ref.shape[2]
    left = prototypes_ref[own_rows(place_ref, own), :]
    mine = cols_ref[:, own_rows(place_ref, own)]
    total = down(mine[V[2] : V[2] + 1, :], out_ref.shape[1]) * weighted_ref[...]
    for i in range(dx_ref.shape[0]):
        at = slice(i * rows, (i + 1) * rows)
        right = features_ref[at, :]
        total = total + product(known_ref[:, at] + exponential(left, right) * dx_ref[i], right)
    out_ref[...] = sharpness * total


def gather_rows_body(ref, out_ref):
    count = ref.shape[0]
    width = out_ref.shape[1]
    for r in range(out_ref.shape[0] // count):
        out_ref[r * count : (r + 1) * count, :] = ref[:, 0, r * width : (r + 1) * width]


def exchange(messages, axis):
    return lax.all_to_all(messages, axis, 0, 0, tiled=True)


def together(*arrays):
    return lax.optimization_barrier(arrays)


def per_device(features, prototypes, prior_counts, cotangent):
    rows, width = features.shape
    columns = prototypes.shape[0]
    samples = lax.axis_size("dp")
    classes = lax.axis_size("cls")
    own = columns // samples
    rows_all = rows * samples
    protos_all = float(columns * classes)
    sliced = rows * width // classes
    counts = prior_counts.reshape(1, columns)
    dp_place = lax.axis_index("dp").astype(jnp.int32).reshape(1)
    cls_place = lax.axis_index("cls").astype(jnp.int32).reshape(1)
    once = 2 * rows * columns
    full = once * width

    cols_t, rws_t, every_t = f32(8, columns), f32(16, rows), f32(8, rows_all)
    to_rows = f32(classes, 1, rows)
    to_columns = f32(samples, 1, columns + rows)
    block_t = f32(rows, columns)

    features_all = lax.all_gather(features, "dp", axis=0, tiled=True)
    kernel, cols, message = call(
        start_body, [block_t, cols_t, f32(classes, 1, rows + LANES + sliced)], [features, prototypes, counts], "start", flops=3 * full
    )
    message = exchange(message, "cls")
    cols, rws, every, message = call(
        functools.partial(columns_first_body, float(rows_all)), [cols_t, rws_t, every_t, to_columns], [message, kernel, cols],
        "columns_first", flops=once,
    )
    message = exchange(message, "dp")
    cols, every, message = call(
        functools.partial(rows_body, 0), [cols_t, every_t, to_rows], [message, kernel, cols, every], "rows_0", flops=once
    )
    message = exchange(message, "cls")
    rws, message = call(functools.partial(columns_body, 1), [rws_t, to_columns], [message, kernel, rws], "columns_1", flops=once)
    message = exchange(message, "dp")
    cols, every, message = call(
        functools.partial(rows_body, 1), [cols_t, every_t, to_rows], [message, kernel, cols, every], "rows_1", flops=once
    )
    message = exchange(message, "cls")
    rws, message = call(
        functools.partial(columns_last_body, 2, protos_all), [rws_t, f32(samples, 1, 2 * columns + rows)],
        [message, kernel, cotangent, rws], "columns_last", flops=2 * once,
    )
    message = exchange(message, "dp")
    cols, every, message = call(
        functools.partial(rows_last_body, 2, protos_all), [cols_t, every_t, to_rows], [message, kernel, cotangent, cols, every],
        "rows_last", flops=2 * once,
    )

    message, right = together(message, features)
    weighted, known = call(
        functools.partial(cotangent_products_body, protos_all), [f32(columns, width), f32(rows, width)],
        [kernel, cotangent, right, prototypes, cols, rws], "cotangent_products", flops=4 * full,
    )
    message, weighted, known = together(exchange(message, "cls"), weighted, known)
    weighted = lax.psum_scatter(weighted, "dp", scatter_dimension=0, tiled=True)
    rws, message = call(functools.partial(back_columns_body, 2), [rws_t, to_columns], [message, kernel, rws], "back_columns_2", flops=once)
    message = exchange(message, "dp")
    cols, every, message = call(
        functools.partial(back_rows_body, 1), [cols_t, every_t, to_rows], [message, kernel, cols, every], "back_rows_1", flops=once
    )
    message = exchange(message, "cls")
    rws, message = call(functools.partial(back_columns_body, 1), [rws_t, to_columns], [message, kernel, rws], "back_columns_1", flops=once)
    message = exchange(message, "dp")
    cols, every, message = call(
        last_rows_body, [cols_t, every_t, f32(classes, 1, rows + sliced)], [message, kernel, prototypes, known, cols, rws, every],
        "last_rows", flops=2 * full,
    )

    message, every, features_all = together(message, every, features_all)
    (known_columns,) = call(
        known_columns_body, [f32(own, rows_all)], [dp_place, prototypes, features_all, cols, every], "known_columns", smem=1, flops=full
    )
    message, known_columns = together(exchange(message, "cls"), known_columns)
    dx_message, message = call(
        finish_rows_body, [f32(samples, 1, rows), f32(classes, 1, sliced)], [cls_place, message, rws], "finish_rows", smem=1
    )
    dx1, message = together(exchange(dx_message, "dp"), message)
    gathered = exchange(message, "cls")
    (prototype_grad,) = call(
        finish_columns_body, [f32(own, width)], [dp_place, dx1, known_columns, prototypes, features_all, cols, weighted],
        "finish_columns", smem=1, flops=3 * full,
    )
    gathered, prototype_grad = together(gathered, prototype_grad)
    (feature_grad,) = call(gather_rows_body, [f32(rows, width)], [gathered], "gather_rows")
    return (feature_grad, prototype_grad)


def solution(mesh):
    return jax.shard_map(
        per_device,
        mesh=mesh,
        in_specs=(P("dp", None), P("cls", None), P("cls"), P("dp", "cls")),
        out_specs=(P("dp", None), P(("cls", "dp"), None)),
        check_vma=False,
    )
```

```python
import functools

import jax
import jax.numpy as jnp
from jax import lax
from jax.experimental import pallas as pl
from jax.experimental.pallas import tpu as pltpu
from jax.sharding import PartitionSpec as P

sharpness = 4.0
relax_power = 0.7

LANES = 128
F32 = jnp.float32
BF16 = jnp.bfloat16


def call(body, outs, args, name, smem=0, flops=0):
    specs = [pl.BlockSpec(memory_space=pltpu.SMEM)] * smem
    specs += [pl.BlockSpec(memory_space=pltpu.VMEM)] * (len(args) - smem)
    moved = sum(a.size * a.dtype.itemsize for a in (*args, *outs))
    return pl.pallas_call(
        body,
        out_shape=outs,
        in_specs=specs,
        out_specs=[pl.BlockSpec(memory_space=pltpu.VMEM)] * len(outs),
        compiler_params=pltpu.CompilerParams(vmem_limit_bytes=24 * 2**20),
        cost_estimate=pl.CostEstimate(flops=flops, bytes_accessed=moved, transcendentals=0),
        name=name,
    )(*args)


def f32(*shape):
    return jax.ShapeDtypeStruct(shape, F32)


def tiles(size, width):
    return [slice(start, start + width) for start in range(0, size, width)]


def down(row, width=LANES):
    return jnp.transpose(jnp.broadcast_to(row, (width, row.shape[1])))


def flat(sums):
    return jnp.sum(jnp.transpose(sums), axis=0, keepdims=True)


def copies(row, count):
    return jnp.broadcast_to(row[None], (count,) + row.shape)


def parts(value):
    high = value.astype(BF16)
    return high, (value - high.astype(F32)).astype(BF16)


def rows_of(kernel_ref, weight):
    sums = 0.0
    for at in tiles(kernel_ref.shape[1], LANES):
        sums = sums + kernel_ref[:, at] * weight(at)
    return flat(sums)


def received(ref, start, stop):
    return jnp.sum(ref[:, :, start:stop], axis=0)


V, Y, TARGET, DY = (0, 1, 2), (3, 4), 5, (3, 4, 5)
U, DX, PLAIN = (0, 1, 2), (None, 4, 3), 8


def carry(old_ref, new_ref):
    new_ref[...] = old_ref[...]


def put(ref, row, value):
    ref[row : row + 1, :] = value


def get(ref, row, at=slice(None)):
    return ref[row : row + 1, at]


def exponential(left, right):
    logits = lax.dot_general(left, right, (((1,), (1,)), ((), ())), preferred_element_type=F32)
    return jnp.exp(sharpness * logits)


def start_body(features_ref, prototypes_ref, counts_ref, kernel_ref, cols_ref, out_ref):
    rows = features_ref.shape[0]
    width = 512
    left = features_ref[...]
    sums, plain = 0.0, 0.0
    for at in tiles(prototypes_ref.shape[0], width):
        right = prototypes_ref[at, :]
        block = exponential(left, right)
        kernel_ref[:, at] = block
        for inner in tiles(width, LANES):
            sums = sums + block[:, inner]
        plain = plain + product(block, right)
    out_ref[:, :, :rows] = copies(flat(sums), out_ref.shape[0])
    scatter_rows(sharpness * plain, out_ref, rows + LANES)
    counts = counts_ref[...].astype(F32)
    cols_ref[...] = jnp.zeros_like(cols_ref)
    put(cols_ref, TARGET, counts)
    total = jnp.sum(counts, axis=1, keepdims=True)
    out_ref[:, :, rows : rows + LANES] = jnp.broadcast_to(total[None], (out_ref.shape[0], 1, LANES))


def message_rows(columns, rows):
    return -(-(columns + 2 * rows) // LANES // 16) * 16


def column_sums(kernel_ref, row, out_ref):
    columns = kernel_ref.shape[1]
    wide = down(row)
    values = [jnp.sum(kernel_ref[:, at] * wide, axis=0, keepdims=True) for at in tiles(columns, LANES)]
    for part in parts(row):
        values += [part.astype(F32)[:, at] for at in tiles(row.shape[1], LANES)]
    spare = out_ref.shape[1] - len(values)
    if spare:
        values.append(jnp.zeros((spare, LANES), F32))
    out_ref[...] = copies(jnp.concatenate(values, axis=0).astype(BF16), out_ref.shape[0])


def received_columns(ref, columns, every_ref, every_out, row):
    values = ref[...].astype(F32)
    sums = jnp.sum(values, axis=0)
    carry(every_ref, every_out)
    first = columns // LANES
    count = every_out.shape[1] // ref.shape[0] // LANES
    samples = values[:, first : first + count, :] + values[:, first + count : first + 2 * count, :]
    for i in range(ref.shape[0]):
        for j in range(count):
            at = (i * count + j) * LANES
            every_out[row : row + 1, at : at + LANES] = samples[i, j : j + 1, :]
    return jnp.concatenate([sums[i : i + 1, :] for i in range(first)], axis=1)


def columns_first_body(samples_all, x_ref, kernel_ref, cols_ref, cols_out, rws_out, every_out, out_ref):
    rows = kernel_ref.shape[0]
    u = 1.0 / received(x_ref, 0, rows)
    column_sums(kernel_ref, u, out_ref)
    total = received(x_ref, rows, rows + LANES)[:, :1]
    carry(cols_ref, cols_out)
    put(cols_out, TARGET, samples_all * get(cols_ref, TARGET) / total)
    rws_out[...] = jnp.zeros_like(rws_out)
    put(rws_out, U[0], u)
    for i, at in enumerate(tiles(x_ref.shape[2] - rows - LANES, rows)):
        put(rws_out, PLAIN + i, received(x_ref, rows + LANES + at.start, rows + LANES + at.stop))
    every_out[...] = jnp.zeros_like(every_out)


def columns_body(step, x_ref, kernel_ref, rws_ref, rws_out, out_ref):
    u = 1.0 / received(x_ref, 0, kernel_ref.shape[0])
    carry(rws_ref, rws_out)
    put(rws_out, U[step], u)
    column_sums(kernel_ref, u, out_ref)


def columns_last_body(step, protos_all, x_ref, kernel_ref, cotangent_ref, rws_ref, rws_out, out_ref):
    rows, columns = kernel_ref.shape
    count = out_ref.shape[0]
    u = 1.0 / received(x_ref, 0, rows)
    carry(rws_ref, rws_out)
    put(rws_out, U[step], u)
    wide = down(u)
    for at in tiles(columns, LANES):
        weighted = kernel_ref[:, at] * wide
        out_ref[:, :, at] = copies(jnp.sum(weighted, axis=0, keepdims=True), count)
        weighted = weighted * cotangent_ref[:, at].astype(F32)
        later = slice(columns + at.start, columns + at.stop)
        out_ref[:, :, later] = copies(protos_all * jnp.sum(weighted, axis=0, keepdims=True), count)
    out_ref[:, :, 2 * columns :] = copies(u, count)


def spread(ref, every_ref, every_out, row, start):
    carry(every_ref, every_out)
    rows = every_out.shape[1] // ref.shape[0]
    for i in range(ref.shape[0]):
        every_out[row : row + 1, i * rows : (i + 1) * rows] = ref[i, :, start : start + rows]


def relaxed(y, cols_ref):
    return jnp.exp(relax_power * jnp.log(get(cols_ref, TARGET) / y))


def rows_body(step, y_ref, kernel_ref, cols_ref, every_ref, cols_out, every_out, out_ref):
    y = received_columns(y_ref, kernel_ref.shape[1], every_ref, every_out, U[step])
    carry(cols_ref, cols_out)
    put(cols_out, Y[step], y)
    put(cols_out, V[step], relaxed(y, cols_ref))
    out_ref[...] = copies(rows_of(kernel_ref, lambda at: get(cols_out, V[step], at)), out_ref.shape[0])


def rows_last_body(step, protos_all, y_ref, kernel_ref, cotangent_ref, cols_ref, every_ref, cols_out, every_out, out_ref):
    columns = kernel_ref.shape[1]
    y = received(y_ref, 0, columns)
    v = relaxed(y, cols_ref)
    carry(cols_ref, cols_out)
    put(cols_out, V[step], v)
    put(cols_out, DY[step], -relax_power * received(y_ref, columns, 2 * columns) * v / y)
    spread(y_ref, every_ref, every_out, U[step], 2 * columns)

    def weight(at):
        return protos_all * cotangent_ref[:, at].astype(F32) * get(cols_out, V[step], at) + get(cols_out, DY[step], at)

    out_ref[...] = copies(rows_of(kernel_ref, weight), out_ref.shape[0])


def back_columns_body(step, du_ref, kernel_ref, rws_ref, rws_out, out_ref):
    u = get(rws_ref, U[step])
    dx = -received(du_ref, 0, kernel_ref.shape[0]) * u * u
    carry(rws_ref, rws_out)
    put(rws_out, DX[step], dx)
    column_sums(kernel_ref, dx, out_ref)


def column_step(step, dv_ref, cols_ref, every_ref, cols_out, every_out):
    dv = received_columns(dv_ref, cols_ref.shape[1], every_ref, every_out, DX[step + 1])
    carry(cols_ref, cols_out)
    put(cols_out, DY[step], -relax_power * dv * get(cols_ref, V[step]) / get(cols_ref, Y[step]))


def back_rows_body(step, dv_ref, kernel_ref, cols_ref, every_ref, cols_out, every_out, out_ref):
    column_step(step, dv_ref, cols_ref, every_ref, cols_out, every_out)
    out_ref[...] = copies(rows_of(kernel_ref, lambda at: get(cols_out, DY[step], at)), out_ref.shape[0])


def scatter_rows(value, out_ref, start):
    count = out_ref.shape[0]
    width = value.shape[1]
    for r in range(value.shape[0] // count):
        block = value[r * count : (r + 1) * count, :]
        out_ref[:, :, start + r * width : start + (r + 1) * width] = block[:, None, :]


def product(value, right):
    high, low = parts(value)
    return jnp.dot(high, right, preferred_element_type=F32) + jnp.dot(low, right, preferred_element_type=F32)


def cotangent_products_body(
    protos_all, kernel_ref, cotangent_ref, features_ref, prototypes_ref, cols_ref, rws_ref, weighted_ref, known_ref
):
    width = 256
    u3 = down(get(rws_ref, U[2]), width)
    features = features_ref[...]
    rows = (((0,), (0,)), ((), ()))
    total = 0.0
    for at in tiles(kernel_ref.shape[1], width):
        block = kernel_ref[:, at] * u3
        weighted = protos_all * cotangent_ref[:, at].astype(F32) * block
        high, low = parts(weighted)
        weighted_ref[at, :] = lax.dot_general(high, features, rows, preferred_element_type=F32) + lax.dot_general(
            low, features, rows, preferred_element_type=F32
        )
        known = weighted * get(cols_ref, V[2], at) + block * get(cols_ref, DY[2], at)
        total = total + product(known, prototypes_ref[at, :])
    known_ref[...] = total


def last_rows_body(
    dv_ref, kernel_ref, prototypes_ref, known_ref, cols_ref, rws_ref, every_ref, both_ref, out_ref
):
    rows, columns = kernel_ref.shape
    cols_out, every_out = both_ref.at[:8, :columns], both_ref.at[8:, : every_ref.shape[1]]
    column_step(0, dv_ref, cols_ref, every_ref, cols_out, every_out)
    width = 256
    u1, u2, dx2, dx3 = (down(get(rws_ref, row), width) for row in (U[0], U[1], DX[1], DX[2]))
    sums, total = 0.0, known_ref[...]
    for at in tiles(columns, width):
        block = kernel_ref[:, at]
        dy1 = get(cols_out, DY[0], at)
        weighted = block * dy1
        for inner in tiles(width, LANES):
            sums = sums + weighted[:, inner]
        inner = u1 * dy1 + u2 * get(cols_out, DY[1], at) + dx2 * get(cols_out, V[0], at) + dx3 * get(cols_out, V[1], at)
        total = total + product(block * inner, prototypes_ref[at, :])
    out_ref[:, :, :rows] = copies(flat(sums), out_ref.shape[0])
    scatter_rows(sharpness * total, out_ref, rows)


def finish_rows_body(place_ref, du_ref, rws_ref, dx_out_ref, out_ref):
    rows = rws_ref.shape[1]
    u = get(rws_ref, U[0])
    dx = -received(du_ref, 0, rows) * u * u
    dx_out_ref[...] = copies(dx, dx_out_ref.shape[0])
    count = out_ref.shape[0]
    mine = received(du_ref, rows, du_ref.shape[2])
    width = mine.shape[1] * count // rows
    lane = lax.broadcasted_iota(jnp.int32, dx.shape, 1)
    values = []
    for r in range(rows // count):
        row = r * count + place_ref[0]
        value = jnp.sum(jnp.where(lane == row, dx, 0.0), axis=1, keepdims=True)
        value = mine[:, r * width : (r + 1) * width] + value * get(rws_ref, PLAIN + r)
        values += [value[:, at] for at in tiles(width, LANES)]
    out_ref[...] = copies(jnp.concatenate(values, axis=0).astype(BF16), count)


def own_rows(place_ref, size):
    return pl.ds(pl.multiple_of(place_ref[0] * size, size), size)


def known_columns_body(place_ref, prototypes_ref, features_ref, both_ref, out_ref):
    own, samples = out_ref.shape
    cols_ref, every_ref = both_ref.at[:8, :], both_ref.at[8:, :]
    left = prototypes_ref[own_rows(place_ref, own), :]
    mine = cols_ref[:, own_rows(place_ref, own)]
    width = 256
    v1, v2, dy1, dy2, dy3 = (down(mine[row : row + 1, :], width) for row in (V[0], V[1], DY[0], DY[1], DY[2]))
    for at in tiles(samples, width):
        inner = get(every_ref, U[2], at) * dy3 + get(every_ref, DX[2], at) * v2
        inner = inner + get(every_ref, U[1], at) * dy2 + get(every_ref, DX[1], at) * v1 + get(every_ref, U[0], at) * dy1
        out_ref[:, at] = inner * exponential(left, features_ref[at, :])


def finish_columns_body(place_ref, dx_ref, known_ref, prototypes_ref, features_ref, both_ref, weighted_ref, out_ref):
    own = known_ref.shape[0]
    rows = dx_ref.shape[2]
    left = prototypes_ref[own_rows(place_ref, own), :]
    mine = both_ref[:8, own_rows(place_ref, own)]
    total = down(mine[V[2] : V[2] + 1, :], out_ref.shape[1]) * weighted_ref[...]
    for i in range(dx_ref.shape[0]):
        at = slice(i * rows, (i + 1) * rows)
        right = features_ref[at, :]
        total = total + product(known_ref[:, at] + exponential(left, right) * dx_ref[i], right)
    out_ref[...] = sharpness * total


def gather_rows_body(ref, out_ref):
    count = ref.shape[0]
    values = ref[...].astype(F32)
    blocks = tiles(out_ref.shape[1], LANES)
    for i in range(ref.shape[1]):
        r, at = i // len(blocks), blocks[i % len(blocks)]
        out_ref[r * count : (r + 1) * count, at] = values[:, i, :]


def exchange(messages, axis):
    return lax.all_to_all(messages, axis, 0, 0, tiled=True)


def together(*arrays):
    return lax.optimization_barrier(arrays)


def per_device(features, prototypes, prior_counts, cotangent):
    rows, width = features.shape
    columns = prototypes.shape[0]
    samples = lax.axis_size("dp")
    classes = lax.axis_size("cls")
    own = columns // samples
    rows_all = rows * samples
    protos_all = float(columns * classes)
    sliced = rows * width // classes
    counts = prior_counts.reshape(1, columns)
    dp_place = lax.axis_index("dp").astype(jnp.int32).reshape(1)
    cls_place = lax.axis_index("cls").astype(jnp.int32).reshape(1)
    once = 2 * rows * columns
    full = once * width

    cols_t, rws_t, every_t = f32(8, columns), f32(16, rows), f32(8, rows_all)
    to_rows = f32(classes, 1, rows)
    to_columns = jax.ShapeDtypeStruct((samples, message_rows(columns, rows), LANES), BF16)
    block_t = f32(rows, columns)

    features_all = lax.all_gather(features, "dp", axis=0, tiled=True)
    kernel, cols, message = call(
        start_body, [block_t, cols_t, f32(classes, 1, rows + LANES + sliced)], [features, prototypes, counts], "start", flops=3 * full
    )
    message = exchange(message, "cls")
    cols, rws, every, message = call(
        functools.partial(columns_first_body, float(rows_all)), [cols_t, rws_t, every_t, to_columns], [message, kernel, cols],
        "columns_first", flops=once,
    )
    message = exchange(message, "dp")
    cols, every, message = call(
        functools.partial(rows_body, 0), [cols_t, every_t, to_rows], [message, kernel, cols, every], "rows_0", flops=once
    )
    message = exchange(message, "cls")
    rws, message = call(functools.partial(columns_body, 1), [rws_t, to_columns], [message, kernel, rws], "columns_1", flops=once)
    message = exchange(message, "dp")
    cols, every, message = call(
        functools.partial(rows_body, 1), [cols_t, every_t, to_rows], [message, kernel, cols, every], "rows_1", flops=once
    )
    message = exchange(message, "cls")
    rws, message = call(
        functools.partial(columns_last_body, 2, protos_all), [rws_t, f32(samples, 1, 2 * columns + rows)],
        [message, kernel, cotangent, rws], "columns_last", flops=2 * once,
    )
    message = exchange(message, "dp")
    cols, every, message = call(
        functools.partial(rows_last_body, 2, protos_all), [cols_t, every_t, to_rows], [message, kernel, cotangent, cols, every],
        "rows_last", flops=2 * once,
    )

    message, right = together(message, features)
    weighted, known = call(
        functools.partial(cotangent_products_body, protos_all), [f32(columns, width), f32(rows, width)],
        [kernel, cotangent, right, prototypes, cols, rws], "cotangent_products", flops=4 * full,
    )
    message, weighted, known = together(exchange(message, "cls"), weighted, known)
    weighted = lax.psum_scatter(weighted, "dp", scatter_dimension=0, tiled=True)
    rws, message = call(functools.partial(back_columns_body, 2), [rws_t, to_columns], [message, kernel, rws], "back_columns_2", flops=once)
    message = exchange(message, "dp")
    cols, every, message = call(
        functools.partial(back_rows_body, 1), [cols_t, every_t, to_rows], [message, kernel, cols, every], "back_rows_1", flops=once
    )
    message = exchange(message, "cls")
    rws, message = call(functools.partial(back_columns_body, 1), [rws_t, to_columns], [message, kernel, rws], "back_columns_1", flops=once)
    message = exchange(message, "dp")
    both, message = call(
        last_rows_body, [f32(16, max(columns, rows_all)), f32(classes, 1, rows + sliced)], [message, kernel, prototypes, known, cols, rws, every],
        "last_rows", flops=2 * full,
    )

    message, both, features_all = together(message, both, features_all)
    (known_columns,) = call(
        known_columns_body, [f32(own, rows_all)], [dp_place, prototypes, features_all, both], "known_columns", smem=1, flops=full
    )
    message, known_columns = together(exchange(message, "cls"), known_columns)
    dx_message, message = call(
        finish_rows_body, [f32(samples, 1, rows), jax.ShapeDtypeStruct((classes, sliced // LANES, LANES), BF16)],
        [cls_place, message, rws], "finish_rows", smem=1,
    )
    dx1, message = together(exchange(dx_message, "dp"), message)
    gathered = exchange(message, "cls")
    (prototype_grad,) = call(
        finish_columns_body, [f32(own, width)], [dp_place, dx1, known_columns, prototypes, features_all, both, weighted],
        "finish_columns", smem=1, flops=3 * full,
    )
    gathered, prototype_grad = together(gathered, prototype_grad)
    (feature_grad,) = call(gather_rows_body, [f32(rows, width)], [gathered], "gather_rows")
    return (feature_grad, prototype_grad)


def solution(mesh):
    return jax.shard_map(
        per_device,
        mesh=mesh,
        in_specs=(P("dp", None), P("cls", None), P("cls"), P("dp", "cls")),
        out_specs=(P("dp", None), P(("cls", "dp"), None)),
        check_vma=False,
    )
```

```python
import functools

import jax
import jax.numpy as jnp
from jax import lax
from jax.experimental import pallas as pl
from jax.experimental.pallas import tpu as pltpu
from jax.sharding import PartitionSpec as P

sharpness = 4.0
relax_power = 0.7

LANES = 128
F32 = jnp.float32
BF16 = jnp.bfloat16


def call(body, outs, args, name, smem=0, flops=0):
    specs = [pl.BlockSpec(memory_space=pltpu.SMEM)] * smem
    specs += [pl.BlockSpec(memory_space=pltpu.VMEM)] * (len(args) - smem)
    moved = sum(a.size * a.dtype.itemsize for a in (*args, *outs))
    return pl.pallas_call(
        body,
        out_shape=outs,
        in_specs=specs,
        out_specs=[pl.BlockSpec(memory_space=pltpu.VMEM)] * len(outs),
        compiler_params=pltpu.CompilerParams(vmem_limit_bytes=24 * 2**20),
        cost_estimate=pl.CostEstimate(flops=flops, bytes_accessed=moved, transcendentals=0),
        name=name,
    )(*args)


def f32(*shape):
    return jax.ShapeDtypeStruct(shape, F32)


def tiles(size, width):
    return [slice(start, start + width) for start in range(0, size, width)]


def down(row, width=LANES):
    return jnp.transpose(jnp.broadcast_to(row, (width, row.shape[1])))


def flat(sums):
    return jnp.sum(jnp.transpose(sums), axis=0, keepdims=True)


def copies(row, count):
    return jnp.broadcast_to(row[None], (count,) + row.shape)


def parts(value):
    high = value.astype(BF16)
    return high, (value - high.astype(F32)).astype(BF16)


def rows_of(kernel_ref, weight):
    sums = 0.0
    for at in tiles(kernel_ref.shape[1], LANES):
        sums = sums + kernel_ref[:, at] * weight(at)
    return flat(sums)


def received(ref, start, stop):
    return jnp.sum(ref[:, :, start:stop], axis=0)


V, Y, TARGET, DY = (0, 1, 2), (3, 4), 5, (3, 4, 5)
U, DX, PLAIN = (0, 1, 2), (None, 4, 3), 8


def carry(old_ref, new_ref):
    new_ref[...] = old_ref[...]


def put(ref, row, value):
    ref[row : row + 1, :] = value


def get(ref, row, at=slice(None)):
    return ref[row : row + 1, at]


def exponential(left, right):
    logits = lax.dot_general(left, right, (((1,), (1,)), ((), ())), preferred_element_type=F32)
    return jnp.exp(sharpness * logits)


def start_body(features_ref, prototypes_ref, counts_ref, kernel_ref, cols_ref, out_ref):
    rows = features_ref.shape[0]
    width = 512
    left = features_ref[...].astype(BF16)
    sums, plain = 0.0, 0.0
    for at in tiles(prototypes_ref.shape[0], width):
        right = prototypes_ref[at, :]
        block = exponential(left, right)
        kernel_ref[:, at] = block
        for inner in tiles(width, LANES):
            sums = sums + block[:, inner]
        plain = plain + product(block, right)
    out_ref[:, :, :rows] = copies(flat(sums), out_ref.shape[0])
    scatter_rows(sharpness * plain, out_ref, rows + LANES)
    counts = counts_ref[...]
    cols_ref[...] = jnp.zeros_like(cols_ref)
    put(cols_ref, TARGET, counts)
    total = jnp.sum(counts, axis=1, keepdims=True)
    out_ref[:, :, rows : rows + LANES] = jnp.broadcast_to(total[None], (out_ref.shape[0], 1, LANES))


def message_rows(columns, rows):
    return -(-(columns + 2 * rows) // LANES // 16) * 16


def column_sums(kernel_ref, row, out_ref):
    columns = kernel_ref.shape[1]
    wide = down(row)
    values = [jnp.sum(kernel_ref[:, at] * wide, axis=0, keepdims=True) for at in tiles(columns, LANES)]
    if out_ref.dtype == F32:
        out_ref[...] = copies(jnp.concatenate([*values, row], axis=1), out_ref.shape[0])
        return
    for part in parts(row):
        values += [part.astype(F32)[:, at] for at in tiles(row.shape[1], LANES)]
    spare = out_ref.shape[1] - len(values)
    if spare:
        values.append(jnp.zeros((spare, LANES), F32))
    out_ref[...] = copies(jnp.concatenate(values, axis=0).astype(BF16), out_ref.shape[0])


def received_columns(ref, columns, every_ref, every_out, row):
    if ref.dtype == F32:
        spread(ref, every_ref, every_out, row, columns)
        return received(ref, 0, columns)
    values = ref[...].astype(F32)
    sums = jnp.sum(values, axis=0)
    carry(every_ref, every_out)
    first = columns // LANES
    count = every_out.shape[1] // ref.shape[0] // LANES
    samples = values[:, first : first + count, :] + values[:, first + count : first + 2 * count, :]
    for i in range(ref.shape[0]):
        for j in range(count):
            at = (i * count + j) * LANES
            every_out[row : row + 1, at : at + LANES] = samples[i, j : j + 1, :]
    return jnp.concatenate([sums[i : i + 1, :] for i in range(first)], axis=1)


def columns_first_body(samples_all, x_ref, kernel_ref, cols_ref, cols_out, rws_out, every_out, out_ref):
    rows = kernel_ref.shape[0]
    u = 1.0 / received(x_ref, 0, rows)
    column_sums(kernel_ref, u, out_ref)
    total = received(x_ref, rows, rows + LANES)[:, :1]
    carry(cols_ref, cols_out)
    put(cols_out, TARGET, samples_all * get(cols_ref, TARGET) / total)
    rws_out[...] = jnp.zeros_like(rws_out)
    put(rws_out, U[0], u)
    for i, at in enumerate(tiles(x_ref.shape[2] - rows - LANES, rows)):
        put(rws_out, PLAIN + i, received(x_ref, rows + LANES + at.start, rows + LANES + at.stop))
    every_out[...] = jnp.zeros_like(every_out)


def columns_body(step, x_ref, kernel_ref, rws_ref, rws_out, out_ref):
    u = 1.0 / received(x_ref, 0, kernel_ref.shape[0])
    carry(rws_ref, rws_out)
    put(rws_out, U[step], u)
    column_sums(kernel_ref, u, out_ref)


def columns_last_body(step, protos_all, x_ref, kernel_ref, cotangent_ref, rws_ref, rws_out, out_ref):
    rows, columns = kernel_ref.shape
    count = out_ref.shape[0]
    u = 1.0 / received(x_ref, 0, rows)
    carry(rws_ref, rws_out)
    put(rws_out, U[step], u)
    wide = down(u)
    for at in tiles(columns, LANES):
        weighted = kernel_ref[:, at] * wide
        out_ref[:, :, at] = copies(jnp.sum(weighted, axis=0, keepdims=True), count)
        weighted = weighted * cotangent_ref[:, at].astype(F32)
        later = slice(columns + at.start, columns + at.stop)
        out_ref[:, :, later] = copies(protos_all * jnp.sum(weighted, axis=0, keepdims=True), count)
    out_ref[:, :, 2 * columns :] = copies(u, count)


def spread(ref, every_ref, every_out, row, start):
    carry(every_ref, every_out)
    rows = every_out.shape[1] // ref.shape[0]
    for i in range(ref.shape[0]):
        every_out[row : row + 1, i * rows : (i + 1) * rows] = ref[i, :, start : start + rows]


def relaxed(y, cols_ref):
    return jnp.exp(relax_power * jnp.log(get(cols_ref, TARGET) / y))


def rows_body(step, y_ref, kernel_ref, cols_ref, every_ref, cols_out, every_out, out_ref):
    y = received_columns(y_ref, kernel_ref.shape[1], every_ref, every_out, U[step])
    carry(cols_ref, cols_out)
    put(cols_out, Y[step], y)
    put(cols_out, V[step], relaxed(y, cols_ref))
    out_ref[...] = copies(rows_of(kernel_ref, lambda at: get(cols_out, V[step], at)), out_ref.shape[0])


def rows_last_body(step, protos_all, y_ref, kernel_ref, cotangent_ref, cols_ref, every_ref, cols_out, every_out, out_ref):
    columns = kernel_ref.shape[1]
    y = received(y_ref, 0, columns)
    v = relaxed(y, cols_ref)
    carry(cols_ref, cols_out)
    put(cols_out, V[step], v)
    put(cols_out, DY[step], -relax_power * received(y_ref, columns, 2 * columns) * v / y)
    spread(y_ref, every_ref, every_out, U[step], 2 * columns)

    def weight(at):
        return protos_all * cotangent_ref[:, at].astype(F32) * get(cols_out, V[step], at) + get(cols_out, DY[step], at)

    out_ref[...] = copies(rows_of(kernel_ref, weight), out_ref.shape[0])


def back_columns_body(step, du_ref, kernel_ref, rws_ref, rws_out, out_ref):
    u = get(rws_ref, U[step])
    dx = -received(du_ref, 0, kernel_ref.shape[0]) * u * u
    carry(rws_ref, rws_out)
    put(rws_out, DX[step], dx)
    column_sums(kernel_ref, dx, out_ref)


def column_step(step, dv_ref, cols_ref, every_ref, cols_out, every_out):
    dv = received_columns(dv_ref, cols_ref.shape[1], every_ref, every_out, DX[step + 1])
    carry(cols_ref, cols_out)
    put(cols_out, DY[step], -relax_power * dv * get(cols_ref, V[step]) / get(cols_ref, Y[step]))


def back_rows_body(step, dv_ref, kernel_ref, cols_ref, every_ref, cols_out, every_out, out_ref):
    column_step(step, dv_ref, cols_ref, every_ref, cols_out, every_out)
    out_ref[...] = copies(rows_of(kernel_ref, lambda at: get(cols_out, DY[step], at)), out_ref.shape[0])


def scatter_rows(value, out_ref, start):
    count = out_ref.shape[0]
    width = value.shape[1]
    for r in range(value.shape[0] // count):
        block = value[r * count : (r + 1) * count, :]
        out_ref[:, :, start + r * width : start + (r + 1) * width] = block[:, None, :]


def product(value, right):
    high, low = parts(value)
    return jnp.dot(high, right, preferred_element_type=F32) + jnp.dot(low, right, preferred_element_type=F32)


def cotangent_products_body(
    protos_all, kernel_ref, cotangent_ref, features_ref, prototypes_ref, cols_ref, rws_ref, weighted_ref, known_ref
):
    width = 256
    u3 = down(get(rws_ref, U[2]), width)
    features = features_ref[...]
    rows = (((0,), (0,)), ((), ()))
    total = 0.0
    for at in tiles(kernel_ref.shape[1], width):
        block = kernel_ref[:, at] * u3
        weighted = protos_all * cotangent_ref[:, at].astype(F32) * block
        high, low = parts(weighted)
        weighted_ref[at, :] = lax.dot_general(high, features, rows, preferred_element_type=F32) + lax.dot_general(
            low, features, rows, preferred_element_type=F32
        )
        known = weighted * get(cols_ref, V[2], at) + block * get(cols_ref, DY[2], at)
        total = total + product(known, prototypes_ref[at, :])
    known_ref[...] = total


def last_rows_body(
    dv_ref, kernel_ref, prototypes_ref, known_ref, cols_ref, rws_ref, every_ref, both_ref, out_ref
):
    rows, columns = kernel_ref.shape
    cols_out, every_out = both_ref.at[:8, :columns], both_ref.at[8:, : every_ref.shape[1]]
    column_step(0, dv_ref, cols_ref, every_ref, cols_out, every_out)
    width = 256
    u1, u2, dx2, dx3 = (down(get(rws_ref, row), width) for row in (U[0], U[1], DX[1], DX[2]))
    sums, total = 0.0, known_ref[...]
    for at in tiles(columns, width):
        block = kernel_ref[:, at]
        dy1 = get(cols_out, DY[0], at)
        weighted = block * dy1
        for inner in tiles(width, LANES):
            sums = sums + weighted[:, inner]
        inner = u1 * dy1 + u2 * get(cols_out, DY[1], at) + dx2 * get(cols_out, V[0], at) + dx3 * get(cols_out, V[1], at)
        total = total + product(block * inner, prototypes_ref[at, :])
    out_ref[:, :, :rows] = copies(flat(sums), out_ref.shape[0])
    scatter_rows(sharpness * total, out_ref, rows)


def finish_rows_body(place_ref, du_ref, rws_ref, dx_out_ref, out_ref):
    rows = rws_ref.shape[1]
    u = get(rws_ref, U[0])
    dx = -received(du_ref, 0, rows) * u * u
    dx_out_ref[...] = copies(dx, dx_out_ref.shape[0])
    count = out_ref.shape[0]
    mine = received(du_ref, rows, du_ref.shape[2])
    width = mine.shape[1] * count // rows
    lane = lax.broadcasted_iota(jnp.int32, dx.shape, 1)
    for r in range(rows // count):
        at = slice(r * width, (r + 1) * width)
        value = jnp.sum(jnp.where(lane == r * count + place_ref[0], dx, 0.0), axis=1, keepdims=True)
        out_ref[:, :, at] = copies(mine[:, at] + value * get(rws_ref, PLAIN + r), count)


def own_rows(place_ref, size):
    return pl.ds(pl.multiple_of(place_ref[0] * size, size), size)


def known_columns_body(place_ref, prototypes_ref, features_ref, both_ref, out_ref):
    own, samples = out_ref.shape
    cols_ref, every_ref = both_ref.at[:8, :], both_ref.at[8:, :]
    left = prototypes_ref[own_rows(place_ref, own), :]
    mine = cols_ref[:, own_rows(place_ref, own)]
    width = 256
    v1, v2, dy1, dy2, dy3 = (down(mine[row : row + 1, :], width) for row in (V[0], V[1], DY[0], DY[1], DY[2]))
    for at in tiles(samples, width):
        inner = get(every_ref, U[2], at) * dy3 + get(every_ref, DX[2], at) * v2
        inner = inner + get(every_ref, U[1], at) * dy2 + get(every_ref, DX[1], at) * v1 + get(every_ref, U[0], at) * dy1
        out_ref[:, at] = inner * exponential(left, features_ref[at, :])


def finish_columns_body(place_ref, dx_ref, known_ref, prototypes_ref, features_ref, both_ref, weighted_ref, out_ref):
    own = known_ref.shape[0]
    rows = dx_ref.shape[2]
    left = prototypes_ref[own_rows(place_ref, own), :]
    mine = both_ref[:8, own_rows(place_ref, own)]
    total = down(mine[V[2] : V[2] + 1, :], out_ref.shape[1]) * weighted_ref[...]
    for i in range(dx_ref.shape[0]):
        at = slice(i * rows, (i + 1) * rows)
        right = features_ref[at, :]
        total = total + product(known_ref[:, at] + exponential(left, right) * dx_ref[i], right)
    out_ref[...] = sharpness * total


def gather_rows_body(ref, out_ref):
    count = ref.shape[0]
    width = out_ref.shape[1]
    for r in range(out_ref.shape[0] // count):
        out_ref[r * count : (r + 1) * count, :] = ref[:, 0, r * width : (r + 1) * width]


def exchange(messages, axis):
    return lax.all_to_all(messages, axis, 0, 0, tiled=True)


def together(*arrays):
    return lax.optimization_barrier(arrays)


def per_device(features, prototypes, prior_counts, cotangent):
    rows, width = features.shape
    columns = prototypes.shape[0]
    samples = lax.axis_size("dp")
    classes = lax.axis_size("cls")
    own = columns // samples
    rows_all = rows * samples
    protos_all = float(columns * classes)
    sliced = rows * width // classes
    counts = prior_counts.astype(F32).reshape(1, columns)
    dp_place = lax.axis_index("dp").astype(jnp.int32).reshape(1)
    cls_place = lax.axis_index("cls").astype(jnp.int32).reshape(1)
    once = 2 * rows * columns
    full = once * width

    cols_t, rws_t, every_t = f32(8, columns), f32(16, rows), f32(8, rows_all)
    to_rows = f32(classes, 1, rows)
    to_columns_exact = f32(samples, 1, columns + rows)
    to_columns = jax.ShapeDtypeStruct((samples, message_rows(columns, rows), LANES), BF16)
    block_t = f32(rows, columns)

    features_all = lax.all_gather(features, "dp", axis=0, tiled=True)
    kernel, cols, message = call(
        start_body, [block_t, cols_t, f32(classes, 1, rows + LANES + sliced)], [features.astype(F32), prototypes, counts], "start", flops=3 * full
    )
    message = exchange(message, "cls")
    cols, rws, every, message = call(
        functools.partial(columns_first_body, float(rows_all)), [cols_t, rws_t, every_t, to_columns], [message, kernel, cols],
        "columns_first", flops=once,
    )
    message = exchange(message, "dp")
    cols, every, message = call(
        functools.partial(rows_body, 0), [cols_t, every_t, to_rows], [message, kernel, cols, every], "rows_0", flops=once
    )
    message = exchange(message, "cls")
    rws, message = call(functools.partial(columns_body, 1), [rws_t, to_columns], [message, kernel, rws], "columns_1", flops=once)
    message = exchange(message, "dp")
    cols, every, message = call(
        functools.partial(rows_body, 1), [cols_t, every_t, to_rows], [message, kernel, cols, every], "rows_1", flops=once
    )
    message = exchange(message, "cls")
    rws, message = call(
        functools.partial(columns_last_body, 2, protos_all), [rws_t, f32(samples, 1, 2 * columns + rows)],
        [message, kernel, cotangent, rws], "columns_last", flops=2 * once,
    )
    message = exchange(message, "dp")
    cols, every, message = call(
        functools.partial(rows_last_body, 2, protos_all), [cols_t, every_t, to_rows], [message, kernel, cotangent, cols, every],
        "rows_last", flops=2 * once,
    )

    message, right = together(message, features)
    weighted, known = call(
        functools.partial(cotangent_products_body, protos_all), [f32(columns, width), f32(rows, width)],
        [kernel, cotangent, right, prototypes, cols, rws], "cotangent_products", flops=4 * full,
    )
    message, weighted, known = together(exchange(message, "cls"), weighted, known)
    weighted = lax.psum_scatter(weighted, "dp", scatter_dimension=0, tiled=True)
    rws, message = call(functools.partial(back_columns_body, 2), [rws_t, to_columns_exact], [message, kernel, rws], "back_columns_2", flops=once)
    message = exchange(message, "dp")
    cols, every, message = call(
        functools.partial(back_rows_body, 1), [cols_t, every_t, to_rows], [message, kernel, cols, every], "back_rows_1", flops=once
    )
    message = exchange(message, "cls")
    rws, message = call(functools.partial(back_columns_body, 1), [rws_t, to_columns], [message, kernel, rws], "back_columns_1", flops=once)
    message = exchange(message, "dp")
    both, message = call(
        last_rows_body, [f32(16, max(columns, rows_all)), f32(classes, 1, rows + sliced)], [message, kernel, prototypes, known, cols, rws, every],
        "last_rows", flops=2 * full,
    )

    message, both, features_all = together(message, both, features_all)
    (known_columns,) = call(
        known_columns_body, [f32(own, rows_all)], [dp_place, prototypes, features_all, both], "known_columns", smem=1, flops=full
    )
    message, known_columns = together(exchange(message, "cls"), known_columns)
    dx_message, message = call(
        finish_rows_body, [f32(samples, 1, rows), f32(classes, 1, sliced)], [cls_place, message, rws], "finish_rows", smem=1
    )
    dx1, message = together(exchange(dx_message, "dp"), message)
    gathered = exchange(message, "cls")
    (prototype_grad,) = call(
        finish_columns_body, [f32(own, width)], [dp_place, dx1, known_columns, prototypes, features_all, both, weighted],
        "finish_columns", smem=1, flops=3 * full,
    )
    gathered, prototype_grad = together(gathered, prototype_grad)
    (feature_grad,) = call(gather_rows_body, [f32(rows, width)], [gathered], "gather_rows")
    return (feature_grad, prototype_grad)


def solution(mesh):
    return jax.shard_map(
        per_device,
        mesh=mesh,
        in_specs=(P("dp", None), P("cls", None), P("cls"), P("dp", "cls")),
        out_specs=(P("dp", None), P(("cls", "dp"), None)),
        check_vma=False,
    )
```

```python
import functools

import jax
import jax.numpy as jnp
from jax import lax
from jax.experimental import pallas as pl
from jax.experimental.pallas import tpu as pltpu
from jax.sharding import PartitionSpec as P

sharpness = 4.0
relax_power = 0.7

LANES = 128
F32 = jnp.float32
BF16 = jnp.bfloat16


def call(body, outs, args, name, smem=0, flops=0):
    specs = [pl.BlockSpec(memory_space=pltpu.SMEM)] * smem
    specs += [pl.BlockSpec(memory_space=pltpu.VMEM)] * (len(args) - smem)
    moved = sum(a.size * a.dtype.itemsize for a in (*args, *outs))
    return pl.pallas_call(
        body,
        out_shape=outs,
        in_specs=specs,
        out_specs=[pl.BlockSpec(memory_space=pltpu.VMEM)] * len(outs),
        compiler_params=pltpu.CompilerParams(vmem_limit_bytes=24 * 2**20),
        cost_estimate=pl.CostEstimate(flops=flops, bytes_accessed=moved, transcendentals=0),
        name=name,
    )(*args)


def f32(*shape):
    return jax.ShapeDtypeStruct(shape, F32)


def tiles(size, width):
    return [slice(start, start + width) for start in range(0, size, width)]


def down(row, width=LANES):
    return jnp.transpose(jnp.broadcast_to(row, (width, row.shape[1])))


def flat(sums):
    return jnp.sum(jnp.transpose(sums), axis=0, keepdims=True)


def copies(row, count):
    return jnp.broadcast_to(row[None], (count,) + row.shape)


def parts(value):
    high = value.astype(BF16)
    return high, (value - high.astype(F32)).astype(BF16)


def rows_of(kernel_ref, weight):
    sums = 0.0
    for at in tiles(kernel_ref.shape[1], LANES):
        sums = sums + kernel_ref[:, at] * weight(at)
    return flat(sums)


def received(ref, start, stop):
    return jnp.sum(ref[:, :, start:stop], axis=0)


V, Y, TARGET, DY = (0, 1, 2), (3, 4), 5, (3, 4, 5)
U, DX, PLAIN = (0, 1, 2), (None, 4, 3), 8


def carry(old_ref, new_ref):
    new_ref[...] = old_ref[...]


def put(ref, row, value):
    ref[row : row + 1, :] = value


def get(ref, row, at=slice(None)):
    return ref[row : row + 1, at]


def exponential(left, right):
    logits = lax.dot_general(left, right, (((1,), (1,)), ((), ())), preferred_element_type=F32)
    return jnp.exp(sharpness * logits)


def start_body(features_ref, prototypes_ref, counts_ref, kernel_ref, cols_ref, out_ref):
    rows = features_ref.shape[0]
    width = 512
    left = features_ref[...].astype(BF16)
    sums, plain = 0.0, 0.0
    for at in tiles(prototypes_ref.shape[0], width):
        right = prototypes_ref[at, :]
        block = exponential(left, right)
        kernel_ref[:, at] = block
        for inner in tiles(width, LANES):
            sums = sums + block[:, inner]
        plain = plain + product(block, right)
    out_ref[:, :, :rows] = copies(flat(sums), out_ref.shape[0])
    scatter_rows(sharpness * plain, out_ref, rows + LANES)
    counts = counts_ref[...]
    cols_ref[...] = jnp.zeros_like(cols_ref)
    put(cols_ref, TARGET, counts)
    total = jnp.sum(counts, axis=1, keepdims=True)
    out_ref[:, :, rows : rows + LANES] = jnp.broadcast_to(total[None], (out_ref.shape[0], 1, LANES))


def message_rows(columns, rows):
    return -(-(columns + 2 * rows) // LANES // 16) * 16


def column_sums(kernel_ref, row, out_ref):
    columns = kernel_ref.shape[1]
    wide = down(row)
    values = [jnp.sum(kernel_ref[:, at] * wide, axis=0, keepdims=True) for at in tiles(columns, LANES)]
    if out_ref.dtype == F32:
        out_ref[...] = copies(jnp.concatenate([*values, row], axis=1), out_ref.shape[0])
        return
    for part in parts(row):
        values += [part.astype(F32)[:, at] for at in tiles(row.shape[1], LANES)]
    spare = out_ref.shape[1] - len(values)
    if spare:
        values.append(jnp.zeros((spare, LANES), F32))
    out_ref[...] = copies(jnp.concatenate(values, axis=0).astype(BF16), out_ref.shape[0])


def received_columns(ref, columns, every_ref, every_out, row):
    if ref.dtype == F32:
        spread(ref, every_ref, every_out, row, columns)
        return received(ref, 0, columns)
    values = ref[...].astype(F32)
    sums = jnp.sum(values, axis=0)
    carry(every_ref, every_out)
    first = columns // LANES
    count = every_out.shape[1] // ref.shape[0] // LANES
    samples = values[:, first : first + count, :] + values[:, first + count : first + 2 * count, :]
    for i in range(ref.shape[0]):
        for j in range(count):
            at = (i * count + j) * LANES
            every_out[row : row + 1, at : at + LANES] = samples[i, j : j + 1, :]
    return jnp.concatenate([sums[i : i + 1, :] for i in range(first)], axis=1)


def columns_first_body(samples_all, x_ref, kernel_ref, cols_ref, cols_out, rws_out, every_out, out_ref):
    rows = kernel_ref.shape[0]
    u = 1.0 / received(x_ref, 0, rows)
    column_sums(kernel_ref, u, out_ref)
    total = received(x_ref, rows, rows + LANES)[:, :1]
    carry(cols_ref, cols_out)
    put(cols_out, TARGET, samples_all * get(cols_ref, TARGET) / total)
    rws_out[...] = jnp.zeros_like(rws_out)
    put(rws_out, U[0], u)
    for i, at in enumerate(tiles(x_ref.shape[2] - rows - LANES, rows)):
        put(rws_out, PLAIN + i, received(x_ref, rows + LANES + at.start, rows + LANES + at.stop))
    every_out[...] = jnp.zeros_like(every_out)


def columns_body(step, x_ref, kernel_ref, rws_ref, rws_out, out_ref):
    u = 1.0 / received(x_ref, 0, kernel_ref.shape[0])
    carry(rws_ref, rws_out)
    put(rws_out, U[step], u)
    column_sums(kernel_ref, u, out_ref)


def columns_last_body(step, protos_all, x_ref, kernel_ref, cotangent_ref, rws_ref, rws_out, out_ref):
    rows, columns = kernel_ref.shape
    count = out_ref.shape[0]
    u = 1.0 / received(x_ref, 0, rows)
    carry(rws_ref, rws_out)
    put(rws_out, U[step], u)
    wide = down(u)
    for at in tiles(columns, LANES):
        weighted = kernel_ref[:, at] * wide
        out_ref[:, :, at] = copies(jnp.sum(weighted, axis=0, keepdims=True), count)
        weighted = weighted * cotangent_ref[:, at].astype(F32)
        later = slice(columns + at.start, columns + at.stop)
        out_ref[:, :, later] = copies(protos_all * jnp.sum(weighted, axis=0, keepdims=True), count)
    out_ref[:, :, 2 * columns :] = copies(u, count)


def spread(ref, every_ref, every_out, row, start):
    carry(every_ref, every_out)
    rows = every_out.shape[1] // ref.shape[0]
    for i in range(ref.shape[0]):
        every_out[row : row + 1, i * rows : (i + 1) * rows] = ref[i, :, start : start + rows]


def relaxed(y, cols_ref):
    return jnp.exp(relax_power * jnp.log(get(cols_ref, TARGET) / y))


def rows_body(step, y_ref, kernel_ref, cols_ref, every_ref, cols_out, every_out, out_ref):
    y = received_columns(y_ref, kernel_ref.shape[1], every_ref, every_out, U[step])
    carry(cols_ref, cols_out)
    put(cols_out, Y[step], y)
    put(cols_out, V[step], relaxed(y, cols_ref))
    out_ref[...] = copies(rows_of(kernel_ref, lambda at: get(cols_out, V[step], at)), out_ref.shape[0])


def rows_last_body(step, protos_all, y_ref, kernel_ref, cotangent_ref, cols_ref, every_ref, cols_out, every_out, out_ref):
    columns = kernel_ref.shape[1]
    y = received(y_ref, 0, columns)
    v = relaxed(y, cols_ref)
    carry(cols_ref, cols_out)
    put(cols_out, V[step], v)
    put(cols_out, DY[step], -relax_power * received(y_ref, columns, 2 * columns) * v / y)
    spread(y_ref, every_ref, every_out, U[step], 2 * columns)

    def weight(at):
        return protos_all * cotangent_ref[:, at].astype(F32) * get(cols_out, V[step], at) + get(cols_out, DY[step], at)

    out_ref[...] = copies(rows_of(kernel_ref, weight), out_ref.shape[0])


def back_columns_body(step, du_ref, kernel_ref, rws_ref, rws_out, out_ref):
    u = get(rws_ref, U[step])
    dx = -received(du_ref, 0, kernel_ref.shape[0]) * u * u
    carry(rws_ref, rws_out)
    put(rws_out, DX[step], dx)
    column_sums(kernel_ref, dx, out_ref)


def column_step(step, dv_ref, cols_ref, every_ref, cols_out, every_out):
    dv = received_columns(dv_ref, cols_ref.shape[1], every_ref, every_out, DX[step + 1])
    carry(cols_ref, cols_out)
    put(cols_out, DY[step], -relax_power * dv * get(cols_ref, V[step]) / get(cols_ref, Y[step]))


def back_rows_body(step, dv_ref, kernel_ref, cols_ref, every_ref, cols_out, every_out, out_ref):
    column_step(step, dv_ref, cols_ref, every_ref, cols_out, every_out)
    out_ref[...] = copies(rows_of(kernel_ref, lambda at: get(cols_out, DY[step], at)), out_ref.shape[0])


def scatter_rows(value, out_ref, start):
    count = out_ref.shape[0]
    width = value.shape[1]
    for r in range(value.shape[0] // count):
        block = value[r * count : (r + 1) * count, :]
        out_ref[:, :, start + r * width : start + (r + 1) * width] = block[:, None, :]


def product(value, right):
    high, low = parts(value)
    return jnp.dot(high, right, preferred_element_type=F32) + jnp.dot(low, right, preferred_element_type=F32)


def cotangent_products_body(
    protos_all, kernel_ref, cotangent_ref, features_ref, prototypes_ref, cols_ref, rws_ref, weighted_ref, known_ref
):
    width = 256
    u3 = down(get(rws_ref, U[2]), width)
    features = features_ref[...]
    rows = (((0,), (0,)), ((), ()))
    total = 0.0
    for at in tiles(kernel_ref.shape[1], width):
        block = kernel_ref[:, at] * u3
        weighted = protos_all * cotangent_ref[:, at].astype(F32) * block
        high, low = parts(weighted)
        weighted_ref[at, :] = lax.dot_general(high, features, rows, preferred_element_type=F32) + lax.dot_general(
            low, features, rows, preferred_element_type=F32
        )
        known = weighted * get(cols_ref, V[2], at) + block * get(cols_ref, DY[2], at)
        total = total + product(known, prototypes_ref[at, :])
    known_ref[...] = total


def last_rows_body(
    dv_ref, kernel_ref, prototypes_ref, known_ref, cols_ref, rws_ref, every_ref, both_ref, out_ref
):
    rows, columns = kernel_ref.shape
    cols_out, every_out = both_ref.at[:8, :columns], both_ref.at[8:, : every_ref.shape[1]]
    column_step(0, dv_ref, cols_ref, every_ref, cols_out, every_out)
    width = 256
    u1, u2, dx2, dx3 = (down(get(rws_ref, row), width) for row in (U[0], U[1], DX[1], DX[2]))
    sums, total = 0.0, known_ref[...]
    for at in tiles(columns, width):
        block = kernel_ref[:, at]
        dy1 = get(cols_out, DY[0], at)
        weighted = block * dy1
        for inner in tiles(width, LANES):
            sums = sums + weighted[:, inner]
        inner = u1 * dy1 + u2 * get(cols_out, DY[1], at) + dx2 * get(cols_out, V[0], at) + dx3 * get(cols_out, V[1], at)
        total = total + product(block * inner, prototypes_ref[at, :])
    out_ref[:, :, :rows] = copies(flat(sums), out_ref.shape[0])
    scatter_rows(sharpness * total, out_ref, rows)


def finish_rows_body(place_ref, du_ref, rws_ref, dx_out_ref, out_ref):
    rows = rws_ref.shape[1]
    u = get(rws_ref, U[0])
    dx = -received(du_ref, 0, rows) * u * u
    dx_out_ref[...] = copies(dx, dx_out_ref.shape[0])
    count = out_ref.shape[0]
    mine = received(du_ref, rows, du_ref.shape[2])
    width = mine.shape[1] * count // rows
    lane = lax.broadcasted_iota(jnp.int32, dx.shape, 1)
    for r in range(rows // count):
        at = slice(r * width, (r + 1) * width)
        value = jnp.sum(jnp.where(lane == r * count + place_ref[0], dx, 0.0), axis=1, keepdims=True)
        out_ref[:, :, at] = copies(mine[:, at] + value * get(rws_ref, PLAIN + r), count)


def own_rows(place_ref, size):
    return pl.ds(pl.multiple_of(place_ref[0] * size, size), size)


def known_columns_body(place_ref, prototypes_ref, features_ref, both_ref, out_ref):
    own, samples = out_ref.shape
    cols_ref, every_ref = both_ref.at[:8, :], both_ref.at[8:, :]
    left = prototypes_ref[own_rows(place_ref, own), :]
    mine = cols_ref[:, own_rows(place_ref, own)]
    width = 256
    v1, v2, dy1, dy2, dy3 = (down(mine[row : row + 1, :], width) for row in (V[0], V[1], DY[0], DY[1], DY[2]))
    for at in tiles(samples, width):
        inner = get(every_ref, U[2], at) * dy3 + get(every_ref, DX[2], at) * v2
        inner = inner + get(every_ref, U[1], at) * dy2 + get(every_ref, DX[1], at) * v1 + get(every_ref, U[0], at) * dy1
        out_ref[:, at] = inner * exponential(left, features_ref[at, :])


def finish_columns_body(place_ref, dx_ref, known_ref, prototypes_ref, features_ref, both_ref, weighted_ref, out_ref):
    own = known_ref.shape[0]
    rows = dx_ref.shape[2]
    left = prototypes_ref[own_rows(place_ref, own), :]
    mine = both_ref[:8, own_rows(place_ref, own)]
    total = down(mine[V[2] : V[2] + 1, :], out_ref.shape[1]) * weighted_ref[...]
    for i in range(dx_ref.shape[0]):
        at = slice(i * rows, (i + 1) * rows)
        right = features_ref[at, :]
        total = total + product(known_ref[:, at] + exponential(left, right) * dx_ref[i], right)
    out_ref[...] = sharpness * total


def gather_rows_body(ref, out_ref):
    count = ref.shape[0]
    width = out_ref.shape[1]
    for r in range(out_ref.shape[0] // count):
        out_ref[r * count : (r + 1) * count, :] = ref[:, 0, r * width : (r + 1) * width]


def exchange(messages, axis):
    return lax.all_to_all(messages, axis, 0, 0, tiled=True)


def together(*arrays):
    return lax.optimization_barrier(arrays)


def per_device(features, prototypes, prior_counts, cotangent):
    rows, width = features.shape
    columns = prototypes.shape[0]
    samples = lax.axis_size("dp")
    classes = lax.axis_size("cls")
    own = columns // samples
    rows_all = rows * samples
    protos_all = float(columns * classes)
    sliced = rows * width // classes
    counts = prior_counts.astype(F32).reshape(1, columns)
    dp_place = lax.axis_index("dp").astype(jnp.int32).reshape(1)
    cls_place = lax.axis_index("cls").astype(jnp.int32).reshape(1)
    once = 2 * rows * columns
    full = once * width

    cols_t, rws_t, every_t = f32(8, columns), f32(16, rows), f32(8, rows_all)
    to_rows = f32(classes, 1, rows)
    to_columns_exact = f32(samples, 1, columns + rows)
    to_columns = jax.ShapeDtypeStruct((samples, message_rows(columns, rows), LANES), BF16)
    block_t = f32(rows, columns)

    features_all = lax.all_gather(features, "dp", axis=0, tiled=True)
    kernel, cols, message = call(
        start_body, [block_t, cols_t, f32(classes, 1, rows + LANES + sliced)], [features.astype(F32), prototypes, counts], "start", flops=3 * full
    )
    message = exchange(message, "cls")
    cols, rws, every, message = call(
        functools.partial(columns_first_body, float(rows_all)), [cols_t, rws_t, every_t, to_columns], [message, kernel, cols],
        "columns_first", flops=once,
    )
    message = exchange(message, "dp")
    cols, every, message = call(
        functools.partial(rows_body, 0), [cols_t, every_t, to_rows], [message, kernel, cols, every], "rows_0", flops=once
    )
    message = exchange(message, "cls")
    rws, message = call(functools.partial(columns_body, 1), [rws_t, to_columns_exact], [message, kernel, rws], "columns_1", flops=once)
    message = exchange(message, "dp")
    cols, every, message = call(
        functools.partial(rows_body, 1), [cols_t, every_t, to_rows], [message, kernel, cols, every], "rows_1", flops=once
    )
    message = exchange(message, "cls")
    rws, message = call(
        functools.partial(columns_last_body, 2, protos_all), [rws_t, f32(samples, 1, 2 * columns + rows)],
        [message, kernel, cotangent, rws], "columns_last", flops=2 * once,
    )
    message = exchange(message, "dp")
    cols, every, message = call(
        functools.partial(rows_last_body, 2, protos_all), [cols_t, every_t, to_rows], [message, kernel, cotangent, cols, every],
        "rows_last", flops=2 * once,
    )

    message, right = together(message, features)
    weighted, known = call(
        functools.partial(cotangent_products_body, protos_all), [f32(columns, width), f32(rows, width)],
        [kernel, cotangent, right, prototypes, cols, rws], "cotangent_products", flops=4 * full,
    )
    message, weighted, known = together(exchange(message, "cls"), weighted, known)
    weighted = lax.psum_scatter(weighted, "dp", scatter_dimension=0, tiled=True)
    rws, message = call(functools.partial(back_columns_body, 2), [rws_t, to_columns_exact], [message, kernel, rws], "back_columns_2", flops=once)
    message = exchange(message, "dp")
    cols, every, message = call(
        functools.partial(back_rows_body, 1), [cols_t, every_t, to_rows], [message, kernel, cols, every], "back_rows_1", flops=once
    )
    message = exchange(message, "cls")
    rws, message = call(functools.partial(back_columns_body, 1), [rws_t, to_columns], [message, kernel, rws], "back_columns_1", flops=once)
    message = exchange(message, "dp")
    both, message = call(
        last_rows_body, [f32(16, max(columns, rows_all)), f32(classes, 1, rows + sliced)], [message, kernel, prototypes, known, cols, rws, every],
        "last_rows", flops=2 * full,
    )

    message, both, features_all = together(message, both, features_all)
    (known_columns,) = call(
        known_columns_body, [f32(own, rows_all)], [dp_place, prototypes, features_all, both], "known_columns", smem=1, flops=full
    )
    message, known_columns = together(exchange(message, "cls"), known_columns)
    dx_message, message = call(
        finish_rows_body, [f32(samples, 1, rows), f32(classes, 1, sliced)], [cls_place, message, rws], "finish_rows", smem=1
    )
    dx1, message = together(exchange(dx_message, "dp"), message)
    gathered = exchange(message, "cls")
    (prototype_grad,) = call(
        finish_columns_body, [f32(own, width)], [dp_place, dx1, known_columns, prototypes, features_all, both, weighted],
        "finish_columns", smem=1, flops=3 * full,
    )
    gathered, prototype_grad = together(gathered, prototype_grad)
    (feature_grad,) = call(gather_rows_body, [f32(rows, width)], [gathered], "gather_rows")
    return (feature_grad, prototype_grad)


def solution(mesh):
    return jax.shard_map(
        per_device,
        mesh=mesh,
        in_specs=(P("dp", None), P("cls", None), P("cls"), P("dp", "cls")),
        out_specs=(P("dp", None), P(("cls", "dp"), None)),
        check_vma=False,
    )
```

```python
import functools

import jax
import jax.numpy as jnp
from jax import lax
from jax.experimental import pallas as pl
from jax.experimental.pallas import tpu as pltpu
from jax.sharding import PartitionSpec as P

sharpness = 4.0
relax_power = 0.7

LANES = 128
F32 = jnp.float32
BF16 = jnp.bfloat16


def call(body, outs, args, name, smem=0, flops=0):
    specs = [pl.BlockSpec(memory_space=pltpu.SMEM)] * smem
    specs += [pl.BlockSpec(memory_space=pltpu.VMEM)] * (len(args) - smem)
    moved = sum(a.size * a.dtype.itemsize for a in (*args, *outs))
    return pl.pallas_call(
        body,
        out_shape=outs,
        in_specs=specs,
        out_specs=[pl.BlockSpec(memory_space=pltpu.VMEM)] * len(outs),
        compiler_params=pltpu.CompilerParams(vmem_limit_bytes=24 * 2**20),
        cost_estimate=pl.CostEstimate(flops=flops, bytes_accessed=moved, transcendentals=0),
        name=name,
    )(*args)


def f32(*shape):
    return jax.ShapeDtypeStruct(shape, F32)


def tiles(size, width):
    return [slice(start, start + width) for start in range(0, size, width)]


def down(row, width=LANES):
    return jnp.transpose(jnp.broadcast_to(row, (width, row.shape[1])))


def flat(sums):
    return jnp.sum(jnp.transpose(sums), axis=0, keepdims=True)


def copies(row, count):
    return jnp.broadcast_to(row[None], (count,) + row.shape)


def parts(value):
    high = value.astype(BF16)
    return high, (value - high.astype(F32)).astype(BF16)


def rows_of(kernel_ref, weight):
    sums = 0.0
    for at in tiles(kernel_ref.shape[1], LANES):
        sums = sums + kernel_ref[:, at] * weight(at)
    return flat(sums)


def received(ref, start, stop):
    return jnp.sum(ref[:, :, start:stop], axis=0)


V, Y, TARGET, DY = (0, 1, 2), (3, 4), 5, (3, 4, 5)
U, DX, PLAIN = (0, 1, 2), (None, 4, 3), 8


def carry(old_ref, new_ref):
    new_ref[...] = old_ref[...]


def put(ref, row, value):
    ref[row : row + 1, :] = value


def get(ref, row, at=slice(None)):
    return ref[row : row + 1, at]


def exponential(left, right):
    logits = lax.dot_general(left, right, (((1,), (1,)), ((), ())), preferred_element_type=F32)
    return jnp.exp(sharpness * logits)


def start_body(features_ref, prototypes_ref, counts_ref, kernel_ref, cols_ref, out_ref):
    rows = features_ref.shape[0]
    width = 512
    left = features_ref[...].astype(BF16)
    sums, plain = 0.0, 0.0
    for at in tiles(prototypes_ref.shape[0], width):
        right = prototypes_ref[at, :]
        block = exponential(left, right)
        kernel_ref[:, at] = block
        for inner in tiles(width, LANES):
            sums = sums + block[:, inner]
        plain = plain + product(block, right)
    out_ref[:, :, :rows] = copies(flat(sums), out_ref.shape[0])
    scatter_rows(sharpness * plain, out_ref, rows + LANES)
    counts = counts_ref[...]
    cols_ref[...] = jnp.zeros_like(cols_ref)
    put(cols_ref, TARGET, counts)
    total = jnp.sum(counts, axis=1, keepdims=True)
    out_ref[:, :, rows : rows + LANES] = jnp.broadcast_to(total[None], (out_ref.shape[0], 1, LANES))


def message_rows(columns, rows):
    return -(-(columns + 2 * rows) // LANES // 16) * 16


def column_sums(kernel_ref, row, out_ref):
    columns = kernel_ref.shape[1]
    wide = down(row)
    values = [jnp.sum(kernel_ref[:, at] * wide, axis=0, keepdims=True) for at in tiles(columns, LANES)]
    if out_ref.dtype == F32:
        out_ref[...] = copies(jnp.concatenate([*values, row], axis=1), out_ref.shape[0])
        return
    for part in parts(row):
        values += [part.astype(F32)[:, at] for at in tiles(row.shape[1], LANES)]
    spare = out_ref.shape[1] - len(values)
    if spare:
        values.append(jnp.zeros((spare, LANES), F32))
    out_ref[...] = copies(jnp.concatenate(values, axis=0).astype(BF16), out_ref.shape[0])


def received_columns(ref, columns, every_ref, every_out, row):
    if ref.dtype == F32:
        spread(ref, every_ref, every_out, row, columns)
        return received(ref, 0, columns)
    values = ref[...].astype(F32)
    sums = jnp.sum(values, axis=0)
    carry(every_ref, every_out)
    first = columns // LANES
    count = every_out.shape[1] // ref.shape[0] // LANES
    samples = values[:, first : first + count, :] + values[:, first + count : first + 2 * count, :]
    for i in range(ref.shape[0]):
        for j in range(count):
            at = (i * count + j) * LANES
            every_out[row : row + 1, at : at + LANES] = samples[i, j : j + 1, :]
    return jnp.concatenate([sums[i : i + 1, :] for i in range(first)], axis=1)


def columns_first_body(samples_all, x_ref, kernel_ref, cols_ref, cols_out, rws_out, every_out, out_ref):
    rows = kernel_ref.shape[0]
    u = 1.0 / received(x_ref, 0, rows)
    column_sums(kernel_ref, u, out_ref)
    total = received(x_ref, rows, rows + LANES)[:, :1]
    carry(cols_ref, cols_out)
    put(cols_out, TARGET, samples_all * get(cols_ref, TARGET) / total)
    rws_out[...] = jnp.zeros_like(rws_out)
    put(rws_out, U[0], u)
    for i, at in enumerate(tiles(x_ref.shape[2] - rows - LANES, rows)):
        put(rws_out, PLAIN + i, received(x_ref, rows + LANES + at.start, rows + LANES + at.stop))
    every_out[...] = jnp.zeros_like(every_out)


def columns_body(step, x_ref, kernel_ref, rws_ref, rws_out, out_ref):
    u = 1.0 / received(x_ref, 0, kernel_ref.shape[0])
    carry(rws_ref, rws_out)
    put(rws_out, U[step], u)
    column_sums(kernel_ref, u, out_ref)


def columns_last_body(step, protos_all, x_ref, kernel_ref, cotangent_ref, rws_ref, rws_out, out_ref):
    rows, columns = kernel_ref.shape
    count = out_ref.shape[0]
    u = 1.0 / received(x_ref, 0, rows)
    carry(rws_ref, rws_out)
    put(rws_out, U[step], u)
    wide = down(u)
    for at in tiles(columns, LANES):
        weighted = kernel_ref[:, at] * wide
        out_ref[:, :, at] = copies(jnp.sum(weighted, axis=0, keepdims=True), count)
        weighted = weighted * cotangent_ref[:, at].astype(F32)
        later = slice(columns + at.start, columns + at.stop)
        out_ref[:, :, later] = copies(protos_all * jnp.sum(weighted, axis=0, keepdims=True), count)
    out_ref[:, :, 2 * columns :] = copies(u, count)


def spread(ref, every_ref, every_out, row, start):
    carry(every_ref, every_out)
    rows = every_out.shape[1] // ref.shape[0]
    for i in range(ref.shape[0]):
        every_out[row : row + 1, i * rows : (i + 1) * rows] = ref[i, :, start : start + rows]


def relaxed(y, cols_ref):
    return jnp.exp(relax_power * jnp.log(get(cols_ref, TARGET) / y))


def rows_body(step, y_ref, kernel_ref, cols_ref, every_ref, cols_out, every_out, out_ref):
    y = received_columns(y_ref, kernel_ref.shape[1], every_ref, every_out, U[step])
    carry(cols_ref, cols_out)
    put(cols_out, Y[step], y)
    put(cols_out, V[step], relaxed(y, cols_ref))
    out_ref[...] = copies(rows_of(kernel_ref, lambda at: get(cols_out, V[step], at)), out_ref.shape[0])


def rows_last_body(step, protos_all, y_ref, kernel_ref, cotangent_ref, cols_ref, every_ref, cols_out, every_out, out_ref):
    columns = kernel_ref.shape[1]
    y = received(y_ref, 0, columns)
    v = relaxed(y, cols_ref)
    carry(cols_ref, cols_out)
    put(cols_out, V[step], v)
    put(cols_out, DY[step], -relax_power * received(y_ref, columns, 2 * columns) * v / y)
    spread(y_ref, every_ref, every_out, U[step], 2 * columns)

    def weight(at):
        return protos_all * cotangent_ref[:, at].astype(F32) * get(cols_out, V[step], at) + get(cols_out, DY[step], at)

    out_ref[...] = copies(rows_of(kernel_ref, weight), out_ref.shape[0])


def back_columns_body(step, du_ref, kernel_ref, rws_ref, rws_out, out_ref):
    u = get(rws_ref, U[step])
    dx = -received(du_ref, 0, kernel_ref.shape[0]) * u * u
    carry(rws_ref, rws_out)
    put(rws_out, DX[step], dx)
    column_sums(kernel_ref, dx, out_ref)


def column_step(step, dv_ref, cols_ref, every_ref, cols_out, every_out):
    dv = received_columns(dv_ref, cols_ref.shape[1], every_ref, every_out, DX[step + 1])
    carry(cols_ref, cols_out)
    put(cols_out, DY[step], -relax_power * dv * get(cols_ref, V[step]) / get(cols_ref, Y[step]))


def back_rows_body(step, dv_ref, kernel_ref, cols_ref, every_ref, cols_out, every_out, out_ref):
    column_step(step, dv_ref, cols_ref, every_ref, cols_out, every_out)
    out_ref[...] = copies(rows_of(kernel_ref, lambda at: get(cols_out, DY[step], at)), out_ref.shape[0])


def scatter_rows(value, out_ref, start):
    count = out_ref.shape[0]
    width = value.shape[1]
    for r in range(value.shape[0] // count):
        block = value[r * count : (r + 1) * count, :]
        out_ref[:, :, start + r * width : start + (r + 1) * width] = block[:, None, :]


def product(value, right):
    high, low = parts(value)
    return jnp.dot(high, right, preferred_element_type=F32) + jnp.dot(low, right, preferred_element_type=F32)


def cotangent_products_body(
    protos_all, kernel_ref, cotangent_ref, features_ref, prototypes_ref, cols_ref, rws_ref, weighted_ref, known_ref
):
    width = 256
    u3 = down(get(rws_ref, U[2]), width)
    features = features_ref[...]
    rows = (((0,), (0,)), ((), ()))
    total = 0.0
    for at in tiles(kernel_ref.shape[1], width):
        block = kernel_ref[:, at] * u3
        weighted = protos_all * cotangent_ref[:, at].astype(F32) * block
        high, low = parts(weighted)
        weighted_ref[at, :] = lax.dot_general(high, features, rows, preferred_element_type=F32) + lax.dot_general(
            low, features, rows, preferred_element_type=F32
        )
        known = weighted * get(cols_ref, V[2], at) + block * get(cols_ref, DY[2], at)
        total = total + product(known, prototypes_ref[at, :])
    known_ref[...] = total


def last_rows_body(
    dv_ref, kernel_ref, prototypes_ref, known_ref, cols_ref, rws_ref, every_ref, both_ref, out_ref
):
    rows, columns = kernel_ref.shape
    cols_out, every_out = both_ref.at[:8, :columns], both_ref.at[8:, : every_ref.shape[1]]
    column_step(0, dv_ref, cols_ref, every_ref, cols_out, every_out)
    width = 256
    u1, u2, dx2, dx3 = (down(get(rws_ref, row), width) for row in (U[0], U[1], DX[1], DX[2]))
    sums, total = 0.0, known_ref[...]
    for at in tiles(columns, width):
        block = kernel_ref[:, at]
        dy1 = get(cols_out, DY[0], at)
        weighted = block * dy1
        for inner in tiles(width, LANES):
            sums = sums + weighted[:, inner]
        inner = u1 * dy1 + u2 * get(cols_out, DY[1], at) + dx2 * get(cols_out, V[0], at) + dx3 * get(cols_out, V[1], at)
        total = total + product(block * inner, prototypes_ref[at, :])
    out_ref[:, :, :rows] = copies(flat(sums), out_ref.shape[0])
    scatter_rows(sharpness * total, out_ref, rows)


def finish_rows_body(place_ref, du_ref, rws_ref, dx_out_ref, out_ref):
    rows = rws_ref.shape[1]
    u = get(rws_ref, U[0])
    dx = -received(du_ref, 0, rows) * u * u
    dx_out_ref[...] = copies(dx, dx_out_ref.shape[0])
    count = out_ref.shape[0]
    mine = received(du_ref, rows, du_ref.shape[2])
    width = mine.shape[1] * count // rows
    lane = lax.broadcasted_iota(jnp.int32, dx.shape, 1)
    for r in range(rows // count):
        at = slice(r * width, (r + 1) * width)
        value = jnp.sum(jnp.where(lane == r * count + place_ref[0], dx, 0.0), axis=1, keepdims=True)
        out_ref[:, :, at] = copies(mine[:, at] + value * get(rws_ref, PLAIN + r), count)


def own_rows(place_ref, size):
    return pl.ds(pl.multiple_of(place_ref[0] * size, size), size)


def known_columns_body(place_ref, prototypes_ref, features_ref, both_ref, out_ref):
    own, samples = out_ref.shape
    cols_ref, every_ref = both_ref.at[:8, :], both_ref.at[8:, :]
    left = prototypes_ref[own_rows(place_ref, own), :]
    mine = cols_ref[:, own_rows(place_ref, own)]
    width = 256
    v1, v2, dy1, dy2, dy3 = (down(mine[row : row + 1, :], width) for row in (V[0], V[1], DY[0], DY[1], DY[2]))
    for at in tiles(samples, width):
        inner = get(every_ref, U[2], at) * dy3 + get(every_ref, DX[2], at) * v2
        inner = inner + get(every_ref, U[1], at) * dy2 + get(every_ref, DX[1], at) * v1 + get(every_ref, U[0], at) * dy1
        out_ref[:, at] = inner * exponential(left, features_ref[at, :])


def finish_columns_body(place_ref, dx_ref, known_ref, prototypes_ref, features_ref, both_ref, weighted_ref, out_ref):
    own = known_ref.shape[0]
    rows = dx_ref.shape[2]
    left = prototypes_ref[own_rows(place_ref, own), :]
    mine = both_ref[:8, own_rows(place_ref, own)]
    total = down(mine[V[2] : V[2] + 1, :], out_ref.shape[1]) * weighted_ref[...]
    for i in range(dx_ref.shape[0]):
        at = slice(i * rows, (i + 1) * rows)
        right = features_ref[at, :]
        total = total + product(known_ref[:, at] + exponential(left, right) * dx_ref[i], right)
    out_ref[...] = sharpness * total


def gather_rows_body(ref, out_ref):
    count = ref.shape[0]
    width = out_ref.shape[1]
    for r in range(out_ref.shape[0] // count):
        out_ref[r * count : (r + 1) * count, :] = ref[:, 0, r * width : (r + 1) * width]


def exchange(messages, axis):
    return lax.all_to_all(messages, axis, 0, 0, tiled=True)


def together(*arrays):
    return lax.optimization_barrier(arrays)


def per_device(features, prototypes, prior_counts, cotangent):
    rows, width = features.shape
    columns = prototypes.shape[0]
    samples = lax.axis_size("dp")
    classes = lax.axis_size("cls")
    own = columns // samples
    rows_all = rows * samples
    protos_all = float(columns * classes)
    sliced = rows * width // classes
    counts = prior_counts.astype(F32).reshape(1, columns)
    dp_place = lax.axis_index("dp").astype(jnp.int32).reshape(1)
    cls_place = lax.axis_index("cls").astype(jnp.int32).reshape(1)
    once = 2 * rows * columns
    full = once * width

    cols_t, rws_t, every_t = f32(8, columns), f32(16, rows), f32(8, rows_all)
    to_rows = f32(classes, 1, rows)
    to_columns_exact = f32(samples, 1, columns + rows)
    to_columns = jax.ShapeDtypeStruct((samples, message_rows(columns, rows), LANES), BF16)
    block_t = f32(rows, columns)

    features_all = lax.all_gather(features, "dp", axis=0, tiled=True)
    kernel, cols, message = call(
        start_body, [block_t, cols_t, f32(classes, 1, rows + LANES + sliced)], [features.astype(F32), prototypes, counts], "start", flops=3 * full
    )
    message = exchange(message, "cls")
    cols, rws, every, message = call(
        functools.partial(columns_first_body, float(rows_all)), [cols_t, rws_t, every_t, to_columns], [message, kernel, cols],
        "columns_first", flops=once,
    )
    message = exchange(message, "dp")
    cols, every, message = call(
        functools.partial(rows_body, 0), [cols_t, every_t, to_rows], [message, kernel, cols, every], "rows_0", flops=once
    )
    message = exchange(message, "cls")
    rws, message = call(functools.partial(columns_body, 1), [rws_t, to_columns_exact], [message, kernel, rws], "columns_1", flops=once)
    message = exchange(message, "dp")
    cols, every, message = call(
        functools.partial(rows_body, 1), [cols_t, every_t, to_rows], [message, kernel, cols, every], "rows_1", flops=once
    )
    message = exchange(message, "cls")
    rws, message = call(
        functools.partial(columns_last_body, 2, protos_all), [rws_t, f32(samples, 1, 2 * columns + rows)],
        [message, kernel, cotangent, rws], "columns_last", flops=2 * once,
    )
    message = exchange(message, "dp")
    cols, every, message = call(
        functools.partial(rows_last_body, 2, protos_all), [cols_t, every_t, to_rows], [message, kernel, cotangent, cols, every],
        "rows_last", flops=2 * once,
    )

    message = exchange(message, "cls")
    rws, message = call(functools.partial(back_columns_body, 2), [rws_t, to_columns_exact], [message, kernel, rws], "back_columns_2", flops=once)
    message = exchange(message, "dp")
    cols, every, message = call(
        functools.partial(back_rows_body, 1), [cols_t, every_t, to_rows], [message, kernel, cols, every], "back_rows_1", flops=once
    )
    message, right = together(message, features)
    weighted, known = call(
        functools.partial(cotangent_products_body, protos_all), [f32(columns, width), f32(rows, width)],
        [kernel, cotangent, right, prototypes, cols, rws], "cotangent_products", flops=4 * full,
    )
    message, weighted, known = together(exchange(message, "cls"), weighted, known)
    weighted = lax.psum_scatter(weighted, "dp", scatter_dimension=0, tiled=True)
    rws, message = call(functools.partial(back_columns_body, 1), [rws_t, to_columns], [message, kernel, rws], "back_columns_1", flops=once)
    message = exchange(message, "dp")
    both, message = call(
        last_rows_body, [f32(16, max(columns, rows_all)), f32(classes, 1, rows + sliced)], [message, kernel, prototypes, known, cols, rws, every],
        "last_rows", flops=2 * full,
    )

    message, both, features_all = together(message, both, features_all)
    (known_columns,) = call(
        known_columns_body, [f32(own, rows_all)], [dp_place, prototypes, features_all, both], "known_columns", smem=1, flops=full
    )
    message, known_columns = together(exchange(message, "cls"), known_columns)
    dx_message, message = call(
        finish_rows_body, [f32(samples, 1, rows), f32(classes, 1, sliced)], [cls_place, message, rws], "finish_rows", smem=1
    )
    dx1, message = together(exchange(dx_message, "dp"), message)
    gathered = exchange(message, "cls")
    (prototype_grad,) = call(
        finish_columns_body, [f32(own, width)], [dp_place, dx1, known_columns, prototypes, features_all, both, weighted],
        "finish_columns", smem=1, flops=3 * full,
    )
    gathered, prototype_grad = together(gathered, prototype_grad)
    (feature_grad,) = call(gather_rows_body, [f32(rows, width)], [gathered], "gather_rows")
    return (feature_grad, prototype_grad)


def solution(mesh):
    return jax.shard_map(
        per_device,
        mesh=mesh,
        in_specs=(P("dp", None), P("cls", None), P("cls"), P("dp", "cls")),
        out_specs=(P("dp", None), P(("cls", "dp"), None)),
        check_vma=False,
    )
```

```python
import functools

import jax
import jax.numpy as jnp
from jax import lax
from jax.experimental import pallas as pl
from jax.experimental.pallas import tpu as pltpu
from jax.sharding import PartitionSpec as P

sharpness = 4.0
relax_power = 0.7

LANES = 128
F32 = jnp.float32
BF16 = jnp.bfloat16


def call(body, outs, args, name, smem=0, flops=0):
    specs = [pl.BlockSpec(memory_space=pltpu.SMEM)] * smem
    specs += [pl.BlockSpec(memory_space=pltpu.VMEM)] * (len(args) - smem)
    moved = sum(a.size * a.dtype.itemsize for a in (*args, *outs))
    return pl.pallas_call(
        body,
        out_shape=outs,
        in_specs=specs,
        out_specs=[pl.BlockSpec(memory_space=pltpu.VMEM)] * len(outs),
        compiler_params=pltpu.CompilerParams(vmem_limit_bytes=24 * 2**20),
        cost_estimate=pl.CostEstimate(flops=flops, bytes_accessed=moved, transcendentals=0),
        name=name,
    )(*args)


def f32(*shape):
    return jax.ShapeDtypeStruct(shape, F32)


def tiles(size, width):
    return [slice(start, start + width) for start in range(0, size, width)]


def down(row, width=LANES):
    return jnp.transpose(jnp.broadcast_to(row, (width, row.shape[1])))


def flat(sums):
    return jnp.sum(jnp.transpose(sums), axis=0, keepdims=True)


def copies(row, count):
    return jnp.broadcast_to(row[None], (count,) + row.shape)


def parts(value):
    high = value.astype(BF16)
    return high, (value - high.astype(F32)).astype(BF16)


def rows_of(kernel_ref, weight):
    sums = 0.0
    for at in tiles(kernel_ref.shape[1], LANES):
        sums = sums + kernel_ref[:, at] * weight(at)
    return flat(sums)


def received(ref, start, stop):
    return jnp.sum(ref[:, :, start:stop], axis=0)


V, Y, TARGET, DY = (0, 1, 2), (3, 4), 5, (3, 4, 5)
U, DX, PLAIN = (0, 1, 2), (None, 4, 3), 8


def carry(old_ref, new_ref):
    new_ref[...] = old_ref[...]


def put(ref, row, value):
    ref[row : row + 1, :] = value


def get(ref, row, at=slice(None)):
    return ref[row : row + 1, at]


def exponential(left, right):
    logits = lax.dot_general(left, right, (((1,), (1,)), ((), ())), preferred_element_type=F32)
    return jnp.exp(sharpness * logits)


def start_body(features_ref, prototypes_ref, counts_ref, kernel_ref, cols_ref, out_ref):
    rows = features_ref.shape[0]
    width = 512
    left = features_ref[...].astype(BF16)
    sums, plain = 0.0, 0.0
    for at in tiles(prototypes_ref.shape[0], width):
        right = prototypes_ref[at, :]
        block = exponential(left, right)
        kernel_ref[:, at] = block
        for inner in tiles(width, LANES):
            sums = sums + block[:, inner]
        plain = plain + product(block, right)
    out_ref[:, :, :rows] = copies(flat(sums), out_ref.shape[0])
    scatter_rows(sharpness * plain, out_ref, rows + LANES)
    counts = counts_ref[...]
    cols_ref[...] = jnp.zeros_like(cols_ref)
    put(cols_ref, TARGET, counts)
    total = jnp.sum(counts, axis=1, keepdims=True)
    out_ref[:, :, rows : rows + LANES] = jnp.broadcast_to(total[None], (out_ref.shape[0], 1, LANES))


def message_rows(columns, rows):
    return -(-(columns + 2 * rows) // LANES // 16) * 16


def column_sums(kernel_ref, row, out_ref):
    columns = kernel_ref.shape[1]
    wide = down(row)
    values = [jnp.sum(kernel_ref[:, at] * wide, axis=0, keepdims=True) for at in tiles(columns, LANES)]
    if out_ref.dtype == F32:
        out_ref[...] = copies(jnp.concatenate([*values, row], axis=1), out_ref.shape[0])
        return
    for part in parts(row):
        values += [part.astype(F32)[:, at] for at in tiles(row.shape[1], LANES)]
    spare = out_ref.shape[1] - len(values)
    if spare:
        values.append(jnp.zeros((spare, LANES), F32))
    out_ref[...] = copies(jnp.concatenate(values, axis=0).astype(BF16), out_ref.shape[0])


def received_columns(ref, columns, every_ref, every_out, row):
    if ref.dtype == F32:
        spread(ref, every_ref, every_out, row, columns)
        return received(ref, 0, columns)
    values = ref[...].astype(F32)
    sums = jnp.sum(values, axis=0)
    carry(every_ref, every_out)
    first = columns // LANES
    count = every_out.shape[1] // ref.shape[0] // LANES
    samples = values[:, first : first + count, :] + values[:, first + count : first + 2 * count, :]
    for i in range(ref.shape[0]):
        for j in range(count):
            at = (i * count + j) * LANES
            every_out[row : row + 1, at : at + LANES] = samples[i, j : j + 1, :]
    return jnp.concatenate([sums[i : i + 1, :] for i in range(first)], axis=1)


def columns_first_body(samples_all, x_ref, kernel_ref, cols_ref, cols_out, rws_out, every_out, out_ref):
    rows = kernel_ref.shape[0]
    u = 1.0 / received(x_ref, 0, rows)
    column_sums(kernel_ref, u, out_ref)
    total = received(x_ref, rows, rows + LANES)[:, :1]
    carry(cols_ref, cols_out)
    put(cols_out, TARGET, samples_all * get(cols_ref, TARGET) / total)
    rws_out[...] = jnp.zeros_like(rws_out)
    put(rws_out, U[0], u)
    for i, at in enumerate(tiles(x_ref.shape[2] - rows - LANES, rows)):
        put(rws_out, PLAIN + i, received(x_ref, rows + LANES + at.start, rows + LANES + at.stop))
    every_out[...] = jnp.zeros_like(every_out)


def columns_body(step, x_ref, kernel_ref, rws_ref, rws_out, out_ref):
    u = 1.0 / received(x_ref, 0, kernel_ref.shape[0])
    carry(rws_ref, rws_out)
    put(rws_out, U[step], u)
    column_sums(kernel_ref, u, out_ref)


def columns_last_body(step, protos_all, x_ref, kernel_ref, cotangent_ref, rws_ref, rws_out, out_ref):
    rows, columns = kernel_ref.shape
    count = out_ref.shape[0]
    u = 1.0 / received(x_ref, 0, rows)
    carry(rws_ref, rws_out)
    put(rws_out, U[step], u)
    wide = down(u)
    for at in tiles(columns, LANES):
        weighted = kernel_ref[:, at] * wide
        out_ref[:, :, at] = copies(jnp.sum(weighted, axis=0, keepdims=True), count)
        weighted = weighted * cotangent_ref[:, at].astype(F32)
        later = slice(columns + at.start, columns + at.stop)
        out_ref[:, :, later] = copies(protos_all * jnp.sum(weighted, axis=0, keepdims=True), count)
    out_ref[:, :, 2 * columns :] = copies(u, count)


def spread(ref, every_ref, every_out, row, start):
    carry(every_ref, every_out)
    rows = every_out.shape[1] // ref.shape[0]
    for i in range(ref.shape[0]):
        every_out[row : row + 1, i * rows : (i + 1) * rows] = ref[i, :, start : start + rows]


def relaxed(y, cols_ref):
    return jnp.exp(relax_power * jnp.log(get(cols_ref, TARGET) / y))


def rows_body(step, y_ref, kernel_ref, cols_ref, every_ref, cols_out, every_out, out_ref):
    y = received_columns(y_ref, kernel_ref.shape[1], every_ref, every_out, U[step])
    carry(cols_ref, cols_out)
    put(cols_out, Y[step], y)
    put(cols_out, V[step], relaxed(y, cols_ref))
    out_ref[...] = copies(rows_of(kernel_ref, lambda at: get(cols_out, V[step], at)), out_ref.shape[0])


def rows_last_body(step, protos_all, y_ref, kernel_ref, cotangent_ref, cols_ref, every_ref, cols_out, every_out, out_ref):
    columns = kernel_ref.shape[1]
    y = received(y_ref, 0, columns)
    v = relaxed(y, cols_ref)
    carry(cols_ref, cols_out)
    put(cols_out, V[step], v)
    put(cols_out, DY[step], -relax_power * received(y_ref, columns, 2 * columns) * v / y)
    spread(y_ref, every_ref, every_out, U[step], 2 * columns)

    def weight(at):
        return protos_all * cotangent_ref[:, at].astype(F32) * get(cols_out, V[step], at) + get(cols_out, DY[step], at)

    out_ref[...] = copies(rows_of(kernel_ref, weight), out_ref.shape[0])


def back_columns_body(step, du_ref, kernel_ref, rws_ref, rws_out, out_ref):
    u = get(rws_ref, U[step])
    dx = -received(du_ref, 0, kernel_ref.shape[0]) * u * u
    carry(rws_ref, rws_out)
    put(rws_out, DX[step], dx)
    column_sums(kernel_ref, dx, out_ref)


def column_step(step, dv_ref, cols_ref, every_ref, cols_out, every_out):
    dv = received_columns(dv_ref, cols_ref.shape[1], every_ref, every_out, DX[step + 1])
    carry(cols_ref, cols_out)
    put(cols_out, DY[step], -relax_power * dv * get(cols_ref, V[step]) / get(cols_ref, Y[step]))


def back_rows_body(step, dv_ref, kernel_ref, cols_ref, every_ref, cols_out, every_out, out_ref):
    column_step(step, dv_ref, cols_ref, every_ref, cols_out, every_out)
    out_ref[...] = copies(rows_of(kernel_ref, lambda at: get(cols_out, DY[step], at)), out_ref.shape[0])


def scatter_rows(value, out_ref, start):
    count = out_ref.shape[0]
    width = value.shape[1]
    for r in range(value.shape[0] // count):
        block = value[r * count : (r + 1) * count, :]
        out_ref[:, :, start + r * width : start + (r + 1) * width] = block[:, None, :]


def product(value, right):
    high, low = parts(value)
    return jnp.dot(high, right, preferred_element_type=F32) + jnp.dot(low, right, preferred_element_type=F32)


def cotangent_products_body(
    protos_all, kernel_ref, cotangent_ref, features_ref, prototypes_ref, cols_ref, rws_ref, weighted_ref, known_ref
):
    width = 256
    u3 = down(get(rws_ref, U[2]), width)
    features = features_ref[...]
    rows = (((0,), (0,)), ((), ()))
    total = 0.0
    for at in tiles(kernel_ref.shape[1], width):
        block = kernel_ref[:, at] * u3
        weighted = protos_all * cotangent_ref[:, at].astype(F32) * block
        high, low = parts(weighted)
        weighted_ref[at, :] = lax.dot_general(high, features, rows, preferred_element_type=F32) + lax.dot_general(
            low, features, rows, preferred_element_type=F32
        )
        known = weighted * get(cols_ref, V[2], at) + block * get(cols_ref, DY[2], at)
        total = total + product(known, prototypes_ref[at, :])
    known_ref[...] = total


def last_rows_body(
    dv_ref, kernel_ref, prototypes_ref, known_ref, cols_ref, rws_ref, every_ref, both_ref, out_ref
):
    rows, columns = kernel_ref.shape
    cols_out, every_out = both_ref.at[:8, :columns], both_ref.at[8:, : every_ref.shape[1]]
    column_step(0, dv_ref, cols_ref, every_ref, cols_out, every_out)
    width = 256
    u1, u2, dx2, dx3 = (down(get(rws_ref, row), width) for row in (U[0], U[1], DX[1], DX[2]))
    sums, total = 0.0, known_ref[...]
    for at in tiles(columns, width):
        block = kernel_ref[:, at]
        dy1 = get(cols_out, DY[0], at)
        weighted = block * dy1
        for inner in tiles(width, LANES):
            sums = sums + weighted[:, inner]
        inner = u1 * dy1 + u2 * get(cols_out, DY[1], at) + dx2 * get(cols_out, V[0], at) + dx3 * get(cols_out, V[1], at)
        total = total + product(block * inner, prototypes_ref[at, :])
    out_ref[:, :, :rows] = copies(flat(sums), out_ref.shape[0])
    scatter_rows(sharpness * total, out_ref, rows)


def finish_rows_body(place_ref, du_ref, rws_ref, dx_out_ref, out_ref):
    rows = rws_ref.shape[1]
    u = get(rws_ref, U[0])
    dx = -received(du_ref, 0, rows) * u * u
    dx_out_ref[...] = copies(dx, dx_out_ref.shape[0])
    count = out_ref.shape[0]
    mine = received(du_ref, rows, du_ref.shape[2])
    width = mine.shape[1] * count // rows
    lane = lax.broadcasted_iota(jnp.int32, dx.shape, 1)
    for r in range(rows // count):
        at = slice(r * width, (r + 1) * width)
        value = jnp.sum(jnp.where(lane == r * count + place_ref[0], dx, 0.0), axis=1, keepdims=True)
        out_ref[:, :, at] = copies(mine[:, at] + value * get(rws_ref, PLAIN + r), count)


def own_rows(place_ref, size):
    return pl.ds(pl.multiple_of(place_ref[0] * size, size), size)


def finish_columns_body(place_ref, dx_ref, prototypes_ref, features_ref, both_ref, weighted_ref, out_ref):
    own = out_ref.shape[0]
    rows = dx_ref.shape[2]
    every_ref = both_ref.at[8:, :]
    left = prototypes_ref[own_rows(place_ref, own), :]
    mine = both_ref[:8, own_rows(place_ref, own)]
    v1, v2, v3, dy1, dy2, dy3 = (down(mine[row : row + 1, :], rows) for row in (*V, *DY))
    total = v3 * weighted_ref[...]
    for i in range(dx_ref.shape[0]):
        at = slice(i * rows, (i + 1) * rows)
        right = features_ref[at, :]
        inner = get(every_ref, U[2], at) * dy3 + get(every_ref, DX[2], at) * v2
        inner = inner + get(every_ref, U[1], at) * dy2 + get(every_ref, DX[1], at) * v1 + get(every_ref, U[0], at) * dy1
        total = total + product((inner + dx_ref[i]) * exponential(left, right), right)
    out_ref[...] = sharpness * total


def gather_rows_body(ref, out_ref):
    count = ref.shape[0]
    width = out_ref.shape[1]
    for r in range(out_ref.shape[0] // count):
        out_ref[r * count : (r + 1) * count, :] = ref[:, 0, r * width : (r + 1) * width]


def exchange(messages, axis):
    return lax.all_to_all(messages, axis, 0, 0, tiled=True)


def together(*arrays):
    return lax.optimization_barrier(arrays)


def per_device(features, prototypes, prior_counts, cotangent):
    rows, width = features.shape
    columns = prototypes.shape[0]
    samples = lax.axis_size("dp")
    classes = lax.axis_size("cls")
    own = columns // samples
    rows_all = rows * samples
    protos_all = float(columns * classes)
    sliced = rows * width // classes
    counts = prior_counts.astype(F32).reshape(1, columns)
    dp_place = lax.axis_index("dp").astype(jnp.int32).reshape(1)
    cls_place = lax.axis_index("cls").astype(jnp.int32).reshape(1)
    once = 2 * rows * columns
    full = once * width

    cols_t, rws_t, every_t = f32(8, columns), f32(16, rows), f32(8, rows_all)
    to_rows = f32(classes, 1, rows)
    to_columns_exact = f32(samples, 1, columns + rows)
    to_columns = jax.ShapeDtypeStruct((samples, message_rows(columns, rows), LANES), BF16)
    block_t = f32(rows, columns)

    features_all = lax.all_gather(features, "dp", axis=0, tiled=True)
    kernel, cols, message = call(
        start_body, [block_t, cols_t, f32(classes, 1, rows + LANES + sliced)], [features.astype(F32), prototypes, counts], "start", flops=3 * full
    )
    message = exchange(message, "cls")
    cols, rws, every, message = call(
        functools.partial(columns_first_body, float(rows_all)), [cols_t, rws_t, every_t, to_columns], [message, kernel, cols],
        "columns_first", flops=once,
    )
    message = exchange(message, "dp")
    cols, every, message = call(
        functools.partial(rows_body, 0), [cols_t, every_t, to_rows], [message, kernel, cols, every], "rows_0", flops=once
    )
    message = exchange(message, "cls")
    rws, message = call(functools.partial(columns_body, 1), [rws_t, to_columns_exact], [message, kernel, rws], "columns_1", flops=once)
    message = exchange(message, "dp")
    cols, every, message = call(
        functools.partial(rows_body, 1), [cols_t, every_t, to_rows], [message, kernel, cols, every], "rows_1", flops=once
    )
    message = exchange(message, "cls")
    rws, message = call(
        functools.partial(columns_last_body, 2, protos_all), [rws_t, f32(samples, 1, 2 * columns + rows)],
        [message, kernel, cotangent, rws], "columns_last", flops=2 * once,
    )
    message = exchange(message, "dp")
    cols, every, message = call(
        functools.partial(rows_last_body, 2, protos_all), [cols_t, every_t, to_rows], [message, kernel, cotangent, cols, every],
        "rows_last", flops=2 * once,
    )

    message, right = together(message, features)
    weighted, known = call(
        functools.partial(cotangent_products_body, protos_all), [f32(columns, width), f32(rows, width)],
        [kernel, cotangent, right, prototypes, cols, rws], "cotangent_products", flops=4 * full,
    )
    message, weighted, known = together(exchange(message, "cls"), weighted, known)
    weighted = lax.psum_scatter(weighted, "dp", scatter_dimension=0, tiled=True)
    rws, message = call(functools.partial(back_columns_body, 2), [rws_t, to_columns_exact], [message, kernel, rws], "back_columns_2", flops=once)
    message = exchange(message, "dp")
    cols, every, message = call(
        functools.partial(back_rows_body, 1), [cols_t, every_t, to_rows], [message, kernel, cols, every], "back_rows_1", flops=once
    )
    message = exchange(message, "cls")
    rws, message = call(functools.partial(back_columns_body, 1), [rws_t, to_columns], [message, kernel, rws], "back_columns_1", flops=once)
    message = exchange(message, "dp")
    both, message = call(
        last_rows_body, [f32(16, max(columns, rows_all)), f32(classes, 1, rows + sliced)], [message, kernel, prototypes, known, cols, rws, every],
        "last_rows", flops=2 * full,
    )

    message = exchange(message, "cls")
    dx_message, message = call(
        finish_rows_body, [f32(samples, 1, rows), f32(classes, 1, sliced)], [cls_place, message, rws], "finish_rows", smem=1
    )
    dx1, message = together(exchange(dx_message, "dp"), message)
    gathered = exchange(message, "cls")
    (prototype_grad,) = call(
        finish_columns_body, [f32(own, width)], [dp_place, dx1, prototypes, features_all, both, weighted],
        "finish_columns", smem=1, flops=3 * full,
    )
    gathered, prototype_grad = together(gathered, prototype_grad)
    (feature_grad,) = call(gather_rows_body, [f32(rows, width)], [gathered], "gather_rows")
    return (feature_grad, prototype_grad)


def solution(mesh):
    return jax.shard_map(
        per_device,
        mesh=mesh,
        in_specs=(P("dp", None), P("cls", None), P("cls"), P("dp", "cls")),
        out_specs=(P("dp", None), P(("cls", "dp"), None)),
        check_vma=False,
    )
```

```python
import functools

import jax
import jax.numpy as jnp
from jax import lax
from jax.experimental import pallas as pl
from jax.experimental.pallas import tpu as pltpu
from jax.sharding import PartitionSpec as P

sharpness = 4.0
relax_power = 0.7

LANES = 128
F32 = jnp.float32
BF16 = jnp.bfloat16


def call(body, outs, args, name, smem=0, flops=0):
    specs = [pl.BlockSpec(memory_space=pltpu.SMEM)] * smem
    specs += [pl.BlockSpec(memory_space=pltpu.VMEM)] * (len(args) - smem)
    moved = sum(a.size * a.dtype.itemsize for a in (*args, *outs))
    return pl.pallas_call(
        body,
        out_shape=outs,
        in_specs=specs,
        out_specs=[pl.BlockSpec(memory_space=pltpu.VMEM)] * len(outs),
        compiler_params=pltpu.CompilerParams(vmem_limit_bytes=24 * 2**20),
        cost_estimate=pl.CostEstimate(flops=flops, bytes_accessed=moved, transcendentals=0),
        name=name,
    )(*args)


def f32(*shape):
    return jax.ShapeDtypeStruct(shape, F32)


def tiles(size, width):
    return [slice(start, start + width) for start in range(0, size, width)]


def down(row, width=LANES):
    return jnp.transpose(jnp.broadcast_to(row, (width, row.shape[1])))


def flat(sums):
    return jnp.sum(jnp.transpose(sums), axis=0, keepdims=True)


def copies(row, count):
    return jnp.broadcast_to(row[None], (count,) + row.shape)


def parts(value):
    high = value.astype(BF16)
    return high, (value - high.astype(F32)).astype(BF16)


def rows_of(kernel_ref, weight):
    sums = 0.0
    for at in tiles(kernel_ref.shape[1], LANES):
        sums = sums + kernel_ref[:, at] * weight(at)
    return flat(sums)


def received(ref, start, stop):
    return jnp.sum(ref[:, :, start:stop], axis=0)


V, Y, TARGET, DY = (0, 1, 2), (3, 4), 5, (3, 4, 5)
U, DX, PLAIN = (0, 1, 2), (None, 4, 3), 8


def carry(old_ref, new_ref):
    new_ref[...] = old_ref[...]


def put(ref, row, value):
    ref[row : row + 1, :] = value


def get(ref, row, at=slice(None)):
    return ref[row : row + 1, at]


def exponential(left, right):
    logits = lax.dot_general(left, right, (((1,), (1,)), ((), ())), preferred_element_type=F32)
    return jnp.exp(sharpness * logits)


def start_body(features_ref, prototypes_ref, counts_ref, kernel_ref, cols_ref, out_ref):
    rows = features_ref.shape[0]
    width = 512
    left = features_ref[...].astype(BF16)
    sums, plain = 0.0, 0.0
    for at in tiles(prototypes_ref.shape[0], width):
        right = prototypes_ref[at, :]
        block = exponential(left, right)
        kernel_ref[:, at] = block
        for inner in tiles(width, LANES):
            sums = sums + block[:, inner]
        plain = plain + product(block, right)
    out_ref[:, :, :rows] = copies(flat(sums), out_ref.shape[0])
    scatter_rows(sharpness * plain, out_ref, rows + LANES)
    counts = counts_ref[...]
    cols_ref[...] = jnp.zeros_like(cols_ref)
    put(cols_ref, TARGET, counts)
    total = jnp.sum(counts, axis=1, keepdims=True)
    out_ref[:, :, rows : rows + LANES] = jnp.broadcast_to(total[None], (out_ref.shape[0], 1, LANES))


def message_rows(columns, rows):
    return -(-(columns + 2 * rows) // LANES // 16) * 16


def column_sums(kernel_ref, row, out_ref):
    columns = kernel_ref.shape[1]
    wide = down(row)
    values = [jnp.sum(kernel_ref[:, at] * wide, axis=0, keepdims=True) for at in tiles(columns, LANES)]
    if out_ref.dtype == F32:
        out_ref[...] = copies(jnp.concatenate([*values, row], axis=1), out_ref.shape[0])
        return
    for part in parts(row):
        values += [part.astype(F32)[:, at] for at in tiles(row.shape[1], LANES)]
    spare = out_ref.shape[1] - len(values)
    if spare:
        values.append(jnp.zeros((spare, LANES), F32))
    out_ref[...] = copies(jnp.concatenate(values, axis=0).astype(BF16), out_ref.shape[0])


def received_columns(ref, columns, every_ref, every_out, row):
    if ref.dtype == F32:
        spread(ref, every_ref, every_out, row, columns)
        return received(ref, 0, columns)
    values = ref[...].astype(F32)
    sums = jnp.sum(values, axis=0)
    carry(every_ref, every_out)
    first = columns // LANES
    count = every_out.shape[1] // ref.shape[0] // LANES
    samples = values[:, first : first + count, :] + values[:, first + count : first + 2 * count, :]
    for i in range(ref.shape[0]):
        for j in range(count):
            at = (i * count + j) * LANES
            every_out[row : row + 1, at : at + LANES] = samples[i, j : j + 1, :]
    return jnp.concatenate([sums[i : i + 1, :] for i in range(first)], axis=1)


def columns_first_body(samples_all, x_ref, kernel_ref, cols_ref, cols_out, rws_out, every_out, out_ref):
    rows = kernel_ref.shape[0]
    u = 1.0 / received(x_ref, 0, rows)
    column_sums(kernel_ref, u, out_ref)
    total = received(x_ref, rows, rows + LANES)[:, :1]
    carry(cols_ref, cols_out)
    put(cols_out, TARGET, samples_all * get(cols_ref, TARGET) / total)
    rws_out[...] = jnp.zeros_like(rws_out)
    put(rws_out, U[0], u)
    for i, at in enumerate(tiles(x_ref.shape[2] - rows - LANES, rows)):
        put(rws_out, PLAIN + i, received(x_ref, rows + LANES + at.start, rows + LANES + at.stop))
    every_out[...] = jnp.zeros_like(every_out)


def columns_body(step, x_ref, kernel_ref, rws_ref, rws_out, out_ref):
    u = 1.0 / received(x_ref, 0, kernel_ref.shape[0])
    carry(rws_ref, rws_out)
    put(rws_out, U[step], u)
    column_sums(kernel_ref, u, out_ref)


def columns_last_body(step, protos_all, x_ref, kernel_ref, cotangent_ref, rws_ref, rws_out, out_ref):
    rows, columns = kernel_ref.shape
    count = out_ref.shape[0]
    u = 1.0 / received(x_ref, 0, rows)
    carry(rws_ref, rws_out)
    put(rws_out, U[step], u)
    wide = down(u)
    for at in tiles(columns, LANES):
        weighted = kernel_ref[:, at] * wide
        out_ref[:, :, at] = copies(jnp.sum(weighted, axis=0, keepdims=True), count)
        weighted = weighted * cotangent_ref[:, at].astype(F32)
        later = slice(columns + at.start, columns + at.stop)
        out_ref[:, :, later] = copies(protos_all * jnp.sum(weighted, axis=0, keepdims=True), count)
    out_ref[:, :, 2 * columns :] = copies(u, count)


def spread(ref, every_ref, every_out, row, start):
    carry(every_ref, every_out)
    rows = every_out.shape[1] // ref.shape[0]
    for i in range(ref.shape[0]):
        every_out[row : row + 1, i * rows : (i + 1) * rows] = ref[i, :, start : start + rows]


def relaxed(y, cols_ref):
    return jnp.exp(relax_power * jnp.log(get(cols_ref, TARGET) / y))


def rows_body(step, y_ref, kernel_ref, cols_ref, every_ref, cols_out, every_out, out_ref):
    y = received_columns(y_ref, kernel_ref.shape[1], every_ref, every_out, U[step])
    carry(cols_ref, cols_out)
    put(cols_out, Y[step], y)
    put(cols_out, V[step], relaxed(y, cols_ref))
    out_ref[...] = copies(rows_of(kernel_ref, lambda at: get(cols_out, V[step], at)), out_ref.shape[0])


def rows_last_body(step, protos_all, y_ref, kernel_ref, cotangent_ref, cols_ref, every_ref, cols_out, every_out, out_ref):
    columns = kernel_ref.shape[1]
    y = received(y_ref, 0, columns)
    v = relaxed(y, cols_ref)
    carry(cols_ref, cols_out)
    put(cols_out, V[step], v)
    put(cols_out, DY[step], -relax_power * received(y_ref, columns, 2 * columns) * v / y)
    spread(y_ref, every_ref, every_out, U[step], 2 * columns)

    def weight(at):
        return protos_all * cotangent_ref[:, at].astype(F32) * get(cols_out, V[step], at) + get(cols_out, DY[step], at)

    out_ref[...] = copies(rows_of(kernel_ref, weight), out_ref.shape[0])


def back_columns_body(step, du_ref, kernel_ref, rws_ref, rws_out, out_ref):
    u = get(rws_ref, U[step])
    dx = -received(du_ref, 0, kernel_ref.shape[0]) * u * u
    carry(rws_ref, rws_out)
    put(rws_out, DX[step], dx)
    column_sums(kernel_ref, dx, out_ref)


def column_step(step, dv_ref, cols_ref, every_ref, cols_out, every_out):
    dv = received_columns(dv_ref, cols_ref.shape[1], every_ref, every_out, DX[step + 1])
    carry(cols_ref, cols_out)
    put(cols_out, DY[step], -relax_power * dv * get(cols_ref, V[step]) / get(cols_ref, Y[step]))


def back_rows_body(step, dv_ref, kernel_ref, cols_ref, every_ref, cols_out, every_out, out_ref):
    column_step(step, dv_ref, cols_ref, every_ref, cols_out, every_out)
    out_ref[...] = copies(rows_of(kernel_ref, lambda at: get(cols_out, DY[step], at)), out_ref.shape[0])


def scatter_rows(value, out_ref, start):
    count = out_ref.shape[0]
    width = value.shape[1]
    for r in range(value.shape[0] // count):
        block = value[r * count : (r + 1) * count, :]
        out_ref[:, :, start + r * width : start + (r + 1) * width] = block[:, None, :]


def product(value, right):
    high, low = parts(value)
    return jnp.dot(high, right, preferred_element_type=F32) + jnp.dot(low, right, preferred_element_type=F32)


def cotangent_products_body(
    protos_all, kernel_ref, cotangent_ref, features_ref, prototypes_ref, cols_ref, rws_ref, weighted_ref, known_ref
):
    width = 256
    u3 = down(get(rws_ref, U[2]), width)
    features = features_ref[...]
    rows = (((0,), (0,)), ((), ()))
    total = 0.0
    for at in tiles(kernel_ref.shape[1], width):
        block = kernel_ref[:, at] * u3
        weighted = protos_all * cotangent_ref[:, at].astype(F32) * block
        high, low = parts(weighted)
        weighted_ref[at, :] = lax.dot_general(high, features, rows, preferred_element_type=F32) + lax.dot_general(
            low, features, rows, preferred_element_type=F32
        )
        known = weighted * get(cols_ref, V[2], at) + block * get(cols_ref, DY[2], at)
        total = total + product(known, prototypes_ref[at, :])
    known_ref[...] = total


def last_rows_body(
    dv_ref, kernel_ref, prototypes_ref, known_ref, cols_ref, rws_ref, every_ref, both_ref, out_ref
):
    rows, columns = kernel_ref.shape
    cols_out, every_out = both_ref.at[:8, :columns], both_ref.at[8:, : every_ref.shape[1]]
    column_step(0, dv_ref, cols_ref, every_ref, cols_out, every_out)
    width = 256
    u1, u2, dx2, dx3 = (down(get(rws_ref, row), width) for row in (U[0], U[1], DX[1], DX[2]))
    sums, total = 0.0, known_ref[...]
    for at in tiles(columns, width):
        block = kernel_ref[:, at]
        dy1 = get(cols_out, DY[0], at)
        weighted = block * dy1
        for inner in tiles(width, LANES):
            sums = sums + weighted[:, inner]
        inner = u1 * dy1 + u2 * get(cols_out, DY[1], at) + dx2 * get(cols_out, V[0], at) + dx3 * get(cols_out, V[1], at)
        total = total + product(block * inner, prototypes_ref[at, :])
    out_ref[:, :, :rows] = copies(flat(sums), out_ref.shape[0])
    scatter_rows(sharpness * total, out_ref, rows)


def finish_rows_body(place_ref, du_ref, rws_ref, dx_out_ref, out_ref):
    rows = rws_ref.shape[1]
    u = get(rws_ref, U[0])
    dx = -received(du_ref, 0, rows) * u * u
    dx_out_ref[...] = copies(dx, dx_out_ref.shape[0])
    count = out_ref.shape[0]
    mine = received(du_ref, rows, du_ref.shape[2])
    width = mine.shape[1] * count // rows
    lane = lax.broadcasted_iota(jnp.int32, dx.shape, 1)
    for r in range(rows // count):
        at = slice(r * width, (r + 1) * width)
        value = jnp.sum(jnp.where(lane == r * count + place_ref[0], dx, 0.0), axis=1, keepdims=True)
        out_ref[:, :, at] = copies(mine[:, at] + value * get(rws_ref, PLAIN + r), count)


def own_rows(place_ref, size):
    return pl.ds(pl.multiple_of(place_ref[0] * size, size), size)


def finish_columns_body(place_ref, dx_ref, prototypes_ref, features_ref, both_ref, weighted_ref, out_ref):
    own = out_ref.shape[0]
    rows = dx_ref.shape[2]
    every_ref = both_ref.at[8:, :]
    left = prototypes_ref[own_rows(place_ref, own), :]
    mine = both_ref[:8, own_rows(place_ref, own)]
    v1, v2, v3, dy1, dy2, dy3 = (down(mine[row : row + 1, :], rows) for row in (*V, *DY))
    total = v3 * weighted_ref[...]
    for i in range(dx_ref.shape[0]):
        at = slice(i * rows, (i + 1) * rows)
        right = features_ref[at, :]
        inner = get(every_ref, U[2], at) * dy3 + get(every_ref, DX[2], at) * v2
        inner = inner + get(every_ref, U[1], at) * dy2 + get(every_ref, DX[1], at) * v1 + get(every_ref, U[0], at) * dy1
        total = total + product((inner + dx_ref[i]) * exponential(left, right), right)
    out_ref[...] = sharpness * total


def gather_rows_body(ref, out_ref):
    count = ref.shape[0]
    width = out_ref.shape[1]
    for r in range(out_ref.shape[0] // count):
        out_ref[r * count : (r + 1) * count, :] = ref[:, 0, r * width : (r + 1) * width]


def exchange(messages, axis):
    return lax.all_to_all(messages, axis, 0, 0, tiled=True)


def together(*arrays):
    return lax.optimization_barrier(arrays)


def per_device(features, prototypes, prior_counts, cotangent):
    rows, width = features.shape
    columns = prototypes.shape[0]
    samples = lax.axis_size("dp")
    classes = lax.axis_size("cls")
    own = columns // samples
    rows_all = rows * samples
    protos_all = float(columns * classes)
    sliced = rows * width // classes
    counts = prior_counts.astype(F32).reshape(1, columns)
    dp_place = lax.axis_index("dp").astype(jnp.int32).reshape(1)
    cls_place = lax.axis_index("cls").astype(jnp.int32).reshape(1)
    once = 2 * rows * columns
    full = once * width

    cols_t, rws_t, every_t = f32(8, columns), f32(16, rows), f32(8, rows_all)
    to_rows = f32(classes, 1, rows)
    to_columns_exact = f32(samples, 1, columns + rows)
    to_columns = jax.ShapeDtypeStruct((samples, message_rows(columns, rows), LANES), BF16)
    block_t = f32(rows, columns)

    features_all = lax.all_gather(features, "dp", axis=0, tiled=True)
    kernel, cols, message = call(
        start_body, [block_t, cols_t, f32(classes, 1, rows + LANES + sliced)], [features.astype(F32), prototypes, counts], "start", flops=3 * full
    )
    message, dp_place, cls_place = together(message, dp_place, cls_place)
    message = exchange(message, "cls")
    cols, rws, every, message = call(
        functools.partial(columns_first_body, float(rows_all)), [cols_t, rws_t, every_t, to_columns], [message, kernel, cols],
        "columns_first", flops=once,
    )
    message = exchange(message, "dp")
    cols, every, message = call(
        functools.partial(rows_body, 0), [cols_t, every_t, to_rows], [message, kernel, cols, every], "rows_0", flops=once
    )
    message = exchange(message, "cls")
    rws, message = call(functools.partial(columns_body, 1), [rws_t, to_columns_exact], [message, kernel, rws], "columns_1", flops=once)
    message = exchange(message, "dp")
    cols, every, message = call(
        functools.partial(rows_body, 1), [cols_t, every_t, to_rows], [message, kernel, cols, every], "rows_1", flops=once
    )
    message = exchange(message, "cls")
    rws, message = call(
        functools.partial(columns_last_body, 2, protos_all), [rws_t, f32(samples, 1, 2 * columns + rows)],
        [message, kernel, cotangent, rws], "columns_last", flops=2 * once,
    )
    message = exchange(message, "dp")
    cols, every, message = call(
        functools.partial(rows_last_body, 2, protos_all), [cols_t, every_t, to_rows], [message, kernel, cotangent, cols, every],
        "rows_last", flops=2 * once,
    )

    message, right = together(message, features)
    weighted, known = call(
        functools.partial(cotangent_products_body, protos_all), [f32(columns, width), f32(rows, width)],
        [kernel, cotangent, right, prototypes, cols, rws], "cotangent_products", flops=4 * full,
    )
    message, weighted, known = together(exchange(message, "cls"), weighted, known)
    weighted = lax.psum_scatter(weighted, "dp", scatter_dimension=0, tiled=True)
    rws, message = call(functools.partial(back_columns_body, 2), [rws_t, to_columns_exact], [message, kernel, rws], "back_columns_2", flops=once)
    message = exchange(message, "dp")
    cols, every, message = call(
        functools.partial(back_rows_body, 1), [cols_t, every_t, to_rows], [message, kernel, cols, every], "back_rows_1", flops=once
    )
    message = exchange(message, "cls")
    rws, message = call(functools.partial(back_columns_body, 1), [rws_t, to_columns], [message, kernel, rws], "back_columns_1", flops=once)
    message = exchange(message, "dp")
    both, message = call(
        last_rows_body, [f32(16, max(columns, rows_all)), f32(classes, 1, rows + sliced)], [message, kernel, prototypes, known, cols, rws, every],
        "last_rows", flops=2 * full,
    )

    message = exchange(message, "cls")
    dx_message, message = call(
        finish_rows_body, [f32(samples, 1, rows), f32(classes, 1, sliced)], [cls_place, message, rws], "finish_rows", smem=1
    )
    dx1, message = together(exchange(dx_message, "dp"), message)
    gathered = exchange(message, "cls")
    (prototype_grad,) = call(
        finish_columns_body, [f32(own, width)], [dp_place, dx1, prototypes, features_all, both, weighted],
        "finish_columns", smem=1, flops=3 * full,
    )
    gathered, prototype_grad = together(gathered, prototype_grad)
    (feature_grad,) = call(gather_rows_body, [f32(rows, width)], [gathered], "gather_rows")
    return (feature_grad, prototype_grad)


def solution(mesh):
    return jax.shard_map(
        per_device,
        mesh=mesh,
        in_specs=(P("dp", None), P("cls", None), P("cls"), P("dp", "cls")),
        out_specs=(P("dp", None), P(("cls", "dp"), None)),
        check_vma=False,
    )
```
